32 devices in a mesh: node: 8 (over z, y), local: 4 (over x, core).
Axes of the slice: x: 2, y: 2, z: 4, core: 2. Of those that a mesh axis runs over, the one named last changes fastest.
Arguments:
- out_grad: bfloat16 [512, 3584], P(('node', 'local')), may hold values from -6 to 6
- saved_input: bfloat16 [512, 3584], P(('node', 'local')), may hold values from -6 to 6
- routes: int32 [512, 8], P(('node', 'local')), may hold values from 0 to 31, as said below
- gate_int: int32 [512, 8], P(('node', 'local')), may hold values from 4096 to 65535
- w_gate: bfloat16 [32, 3584, 1024], P(('node', 'local')), may hold values from -0.09375 to 0.09375
- w_up: bfloat16 [32, 3584, 1024], P(('node', 'local')), may hold values from -0.09375 to 0.09375
- w_down: bfloat16 [32, 1024, 3584], P(('node', 'local')), may hold values from -0.09375 to 0.09375
Outputs:
- input_grad: bfloat16 [512, 3584], P(('node', 'local'))
- gate_grad: bfloat16 [512, 8], P(('node', 'local'))
The draws below stay inside these ranges and needn't reach their ends.
Inputs may be any that keep to these rules, and one draw needn't show every extreme that they name: `routes`: each token names 8 different experts; picks 2 j and 2 j + 1 of a token lie in one node group (expert e is in group e // 4), and the four groups of a token differ. The 16 tokens of one device name one expert at most 4 times and one node group at most 8 times.
All inputs are finite; a program needn't handle non-finite values.
Results may differ from the reference program's by a relative error of at most 0.012.
Values may be sent and summed in bfloat16 or wider, within the bound.
No kernel may reach another device: no remote copies, remote signals or barrier semaphores. Data moves between devices by JAX's collectives and lax.ppermute only.
A program may use at most 128 MiB of HBM per device.

```python
import jax
import jax.numpy as jnp
from jax import lax

D = 3584
F = 1024
TOPK = 8
TOK_DEV = 16
EXPERTS = 32
TOKENS = 512
SLOT = 4
N_NODE = 8
N_LOCAL = 4


def draw_routes(key, part):
    device_total = TOKENS // TOK_DEV
    group_bias = jax.random.randint(jax.random.fold_in(key, 11), (N_NODE,), 0, 4)
    favoured = jax.random.randint(jax.random.fold_in(key, 12), (), 0, N_NODE)
    group_ids = jnp.arange(N_NODE, dtype=jnp.int32)
    group_bias = jnp.where(group_ids == favoured, 8, group_bias)
    half_tokens = TOK_DEV // 2
    cold_blocks = (N_NODE - 4) // 4
    pair_total = N_LOCAL // 2
    column = jnp.arange(4, dtype=jnp.int32)

    def one_device(device):
        device_key = jax.random.fold_in(key, 1000 + device)
        noise_draw = jax.random.randint(jax.random.fold_in(device_key, 1), (N_NODE,), 0, 16384)
        scores = group_bias * 1048576 + noise_draw * 64 + group_ids
        ranking = jnp.argsort(-scores).astype(jnp.int32)
        hot_groups = ranking[:4]
        cold_groups = ranking[4:]
        shuffle = jax.random.permutation(jax.random.fold_in(device_key, 2), N_LOCAL).astype(jnp.int32)
        token_rank = jax.random.permutation(jax.random.fold_in(device_key, 3), TOK_DEV).astype(jnp.int32)
        is_hot = token_rank < half_tokens
        cold_rank = jnp.maximum(token_rank - half_tokens, 0)
        cold_index = (cold_rank % cold_blocks)[:, None] * 4 + column[None, :]
        groups = jnp.where(is_hot[:, None], hot_groups[None, :], cold_groups[cold_index])
        base_rank = jnp.where(is_hot, token_rank, cold_rank // cold_blocks)
        pair_pick = (base_rank[:, None] + column[None, :]) % pair_total
        first_local = shuffle[2 * pair_pick]
        second_local = shuffle[2 * pair_pick + 1]
        experts = jnp.stack([groups * N_LOCAL + first_local, groups * N_LOCAL + second_local], axis=-1)
        return experts.reshape(TOK_DEV, TOPK).astype(jnp.int32)
    return jax.vmap(one_device)(jnp.arange(device_total, dtype=jnp.int32)).reshape(TOKENS, TOPK)


def place_ends(values, key, smallest, high):
    extent = values.shape
    place = [jax.random.randint(jax.random.fold_in(key, axis), (), 0, extent[axis]) for axis in range(len(extent))]
    values = values.at[tuple(place)].set(smallest)
    longest = extent.index(max(extent))
    place[longest] = (place[longest] + 1) % extent[longest]
    return values.at[tuple(place)].set(high)


def block_scale(own_key, shape, cuts, smallest, largest):
    def one(position, shards_of):
        heights = jax.random.uniform(jax.random.fold_in(jax.random.fold_in(own_key, 6), position), (shards_of,), jnp.float32, smallest / len(cuts), largest / len(cuts))
        return jnp.repeat(jnp.exp(heights), shape[position] // shards_of).reshape((-1,) + (1,) * (len(shape) - position - 1))

    gain = one(*cuts[0])
    for cut in cuts[1:]:
        gain = gain * one(*cut)
    return gain


def gaussian(own_key, extent, spread, most, split=(), kind=jnp.bfloat16):
    array = spread * jax.random.normal(own_key, extent, jnp.float32)
    if split:
        array = array * block_scale(own_key, extent, split, -0.22, 0.18)
    return jnp.clip(array, -most, most).astype(kind)


def setup_inputs(seed: int = 0) -> dict:
    streams_of = jax.random.split(jax.random.key(seed), 8)
    out_grad = gaussian(streams_of[0], (TOKENS, D), 1.0, 6.0, ((0, 32),))
    saved_input = gaussian(streams_of[1], (TOKENS, D), 1.0, 6.0, ((0, 32),))
    routes = draw_routes(jax.random.fold_in(streams_of[7], 71), 0)
    gate_int = place_ends(jax.random.randint(streams_of[3], (TOKENS, TOPK), 4096, 65536), jax.random.fold_in(streams_of[3], 1), 4096, 65535).astype(jnp.int32)
    w_gate = gaussian(streams_of[4], (EXPERTS, D, F), D ** -0.5, 0.09375, ((0, 32),))
    w_up = gaussian(streams_of[5], (EXPERTS, D, F), D ** -0.5, 0.09375, ((0, 32),))
    w_down = gaussian(streams_of[6], (EXPERTS, F, D), D ** -0.5, 0.09375, ((0, 32),))
    return {"out_grad": out_grad, "saved_input": saved_input, "routes": routes, "gate_int": gate_int, "w_gate": w_gate, "w_up": w_up, "w_down": w_down}


def expert_backward(input_rows, grad_rows, gate_proj, up_proj, down_proj):
    pre_gate = jnp.dot(input_rows, gate_proj, preferred_element_type=jnp.float32)
    pre_up = jnp.dot(input_rows, up_proj, preferred_element_type=jnp.float32)
    grad_hidden = jnp.dot(grad_rows, down_proj.T, preferred_element_type=jnp.float32)
    sigmoid = jax.nn.sigmoid(pre_gate)
    activated = pre_gate * sigmoid
    gate_score = jnp.sum(activated * pre_up * grad_hidden, axis=-1).astype(jnp.bfloat16)
    grad_gate = (grad_hidden * pre_up * sigmoid * (1.0 + pre_gate * (1.0 - sigmoid))).astype(jnp.bfloat16)
    grad_up = (grad_hidden * activated).astype(jnp.bfloat16)
    row_grad = jnp.dot(grad_gate, gate_proj.T, preferred_element_type=jnp.float32)
    row_grad = row_grad + jnp.dot(grad_up, up_proj.T, preferred_element_type=jnp.float32)
    return row_grad.astype(jnp.bfloat16), gate_score


def reference(out_grad, saved_input, routes, gate_int, w_gate, w_up, w_down):
    token_count = routes.shape[0]
    top_count = routes.shape[1]
    pair_total = token_count * top_count
    feature_width = out_grad.shape[1]
    capacity = N_NODE * N_LOCAL * SLOT
    flat_expert = routes.reshape(-1).astype(jnp.int32)
    order_picks = jnp.argsort(flat_expert, stable=True).astype(jnp.int32)
    sorted_expert = flat_expert[order_picks]
    expert_ids = jnp.arange(EXPERTS, dtype=jnp.int32)
    expert_start = jnp.searchsorted(sorted_expert, expert_ids).astype(jnp.int32)
    expert_count = jnp.sum((flat_expert[None, :] == expert_ids[:, None]).astype(jnp.int32), axis=1)
    gate_flat = gate_int.reshape(-1).astype(jnp.float32) * (1.0 / 65536.0)

    def one_expert(state_pair, expert):
        group_acc, score_acc = state_pair
        offsets = jnp.arange(capacity, dtype=jnp.int32)
        valid_rows = offsets < expert_count[expert]
        pick_index = order_picks[jnp.clip(expert_start[expert] + offsets, 0, pair_total - 1)]
        token_ids = pick_index // top_count
        zero_value = jnp.zeros((), out_grad.dtype)
        input_rows = jnp.where(valid_rows[:, None], saved_input[token_ids], zero_value)
        grad_rows = jnp.where(valid_rows[:, None], out_grad[token_ids], zero_value)
        row_grad, gate_score = expert_backward(input_rows, grad_rows, w_gate[expert], w_up[expert], w_down[expert])
        target = jnp.where(valid_rows, pick_index, pair_total)
        weight = gate_flat[pick_index]
        group_acc = group_acc.at[target // 2].add(row_grad.astype(jnp.float32) * weight[:, None], mode="drop")
        score_acc = score_acc.at[target].set(gate_score, mode="drop")
        return (group_acc, score_acc), None

    start_state = (jnp.zeros((pair_total // 2, feature_width), jnp.float32), jnp.zeros((pair_total,), jnp.bfloat16))
    final_state, unused = lax.scan(one_expert, start_state, expert_ids)
    group_acc, score_acc = final_state
    group_grad = group_acc.astype(jnp.bfloat16).reshape(token_count, top_count // 2, feature_width)
    input_grad = jnp.sum(group_grad.astype(jnp.float32), axis=1).astype(jnp.bfloat16)
    gate_grad = score_acc.reshape(token_count, top_count)
    return input_grad, gate_grad
```

```python
import functools
import math

import jax
import jax.numpy as jnp
from jax import lax
from jax.experimental import pallas as pl
from jax.experimental.pallas import tpu as pltpu
from jax.sharding import Mesh
from jax.sharding import PartitionSpec as P

F32 = jnp.float32
BF16 = jnp.bfloat16
LANES = 128
SLOT = 4
AXES = ("far", "near", "chip", "core")
TN = (((0,), (0,)), ((), ()))
VMEM = pl.BlockSpec(memory_space=pltpu.VMEM)
HBM = pl.BlockSpec(memory_space=pltpu.HBM)
ANY = pl.BlockSpec(memory_space=pl.ANY)
MIB = 2**20
PIECE = 256
COST = pl.CostEstimate(flops=1, bytes_accessed=10_000_000, transcendentals=0)
SMALL = pl.CostEstimate(flops=1, bytes_accessed=1, transcendentals=0)


def iota(shape, dim):
    return lax.broadcasted_iota(jnp.int32, shape, dim)


def exact(mask):
    return mask.astype(F32).astype(BF16)


def in_hbm(array):
    return pltpu.with_memory_space_constraint(array, pltpu.HBM)


def in_vmem(array):
    return pltpu.with_memory_space_constraint(array, pltpu.VMEM)


def unit(count):
    return exact(iota((count, count), 0) == iota((count, count), 1))


def pack_kernel(input_hbm, grad_hbm, routes_hbm, gate_hbm, out_ref, routes_ref, gate_ref, sems):
    width = input_hbm.shape[1]
    copies = [
        pltpu.make_async_copy(routes_hbm, routes_ref, sems.at[0]),
        pltpu.make_async_copy(gate_hbm, gate_ref, sems.at[1]),
        pltpu.make_async_copy(input_hbm, out_ref.at[:, pl.ds(0, width)], sems.at[2]),
        pltpu.make_async_copy(grad_hbm, out_ref.at[:, pl.ds(width + LANES, width)], sems.at[3]),
    ]
    for copy in copies:
        copy.start()
    copies[0].wait()
    copies[1].wait()
    picks = routes_ref.shape[0]
    gate = gate_ref[...]
    table = jnp.concatenate([routes_ref[...], gate // 256, gate % 256], axis=0)
    place = exact(iota((3 * picks, LANES), 0) == iota((3 * picks, LANES), 1))
    out_ref[:, width : width + LANES] = lax.dot_general(
        table.astype(F32).astype(BF16), place, TN, preferred_element_type=F32
    ).astype(BF16)
    copies[2].wait()
    copies[3].wait()


def pack(input_rows, grad_rows, routes_t, gate_t):
    tokens, width = input_rows.shape
    return pl.pallas_call(
        pack_kernel,
        out_shape=jax.ShapeDtypeStruct((tokens, 2 * width + LANES), BF16),
        in_specs=[HBM] * 4,
        out_specs=VMEM,
        scratch_shapes=[
            pltpu.VMEM(routes_t.shape, jnp.int32),
            pltpu.VMEM(gate_t.shape, jnp.int32),
            pltpu.SemaphoreType.DMA((4,)),
        ],
        cost_estimate=SMALL,
        compiler_params=pltpu.CompilerParams(vmem_limit_bytes=4 * MIB),
        name="pack_tokens",
    )(*(in_hbm(a) for a in (input_rows, grad_rows, routes_t, gate_t)))


def choose(meta, chips, picks):
    tokens = meta[0].shape[0]
    blocks = len(meta)
    lines = blocks * SLOT
    names = jnp.concatenate([m[:, :picks] for m in meta], axis=0).astype(F32)
    shape = (blocks * tokens, chips * lines)
    lane, row = iota(shape, 1), iota(shape, 0)
    chip = jnp.bitwise_xor(lane // lines, lax.axis_index("chip"))
    plane = lax.axis_index("far") * 2 + lax.axis_index("near")
    owner = (2 * (plane * chips + chip) + lax.axis_index("core")).astype(F32)
    named = jnp.zeros(shape, F32)
    for k in range(picks):
        named = named + (names[:, k : k + 1] == owner).astype(F32)
    square = (blocks * tokens, blocks * tokens)
    r, c = iota(square, 0), iota(square, 1)
    before = exact(jnp.logical_and(c < r, c // tokens == r // tokens))
    rank = jnp.dot(before, named.astype(BF16), preferred_element_type=F32)
    fits = jnp.logical_and(rank == (lane % SLOT).astype(F32), (lane // SLOT) % blocks == row // tokens)
    return names, owner, jnp.where(fits, named, 0.0)


def dispatch_kernel(kinds, chips, picks, extra, *refs):
    outs = refs[-chips:]
    width = outs[0].shape[1] // 2
    blocks, at = [], 0
    for kind in kinds:
        if kind == 1:
            blocks.append((refs[at], refs[at], width + LANES))
        else:
            blocks.append((refs[at], refs[at + 1], 0))
        at += kind
    meta = [b[0][:, width : width + LANES] for b in blocks]
    _, _, hit = choose(meta, chips, picks)
    pick = hit.astype(BF16)
    lines = len(blocks) * SLOT
    step = math.gcd(width, 512)
    for part in range(2):
        for at in range(0, width, step):
            rows = jnp.concatenate(
                [
                    grads[:, first + at : first + at + step] if part else ins[:, at : at + step]
                    for ins, grads, first in blocks
                ],
                axis=0,
            )
            moved = lax.dot_general(pick, rows, TN, preferred_element_type=F32).astype(BF16)
            for j in range(chips):
                outs[j][:, part * width + at : part * width + at + step] = moved[
                    j * lines : (j + 1) * lines, :
                ]


def dispatch(blocks, chips, picks, after):
    kinds = tuple(len(b) for b in blocks)
    flat = [a for b in blocks for a in b]
    wide = sum(a.shape[1] for a in blocks[0]) - LANES
    lines = len(blocks) * SLOT
    return pl.pallas_call(
        functools.partial(dispatch_kernel, kinds, chips, picks, len(after)),
        out_shape=(jax.ShapeDtypeStruct((lines, wide), BF16),) * chips,
        in_specs=[VMEM] * (len(flat) + len(after)),
        out_specs=(VMEM,) * chips,
        cost_estimate=SMALL,
        compiler_params=pltpu.CompilerParams(vmem_limit_bytes=8 * MIB),
        name="dispatch_rows",
    )(*flat, *(in_vmem(a) for a in after))


def plan_kernel(chips, picks, *refs):
    meta, (weight_ref, mine_ref) = refs[:-2], refs[-2:]
    names, owner, hit = choose([m[...] for m in meta], chips, picks)
    tokens = names.shape[0]
    bytes_of = lambda part: jnp.concatenate(
        [m[:, part * picks : (part + 1) * picks] for m in meta], axis=0
    ).astype(F32)
    high, low = bytes_of(1) * (1.0 / 256.0), bytes_of(2) * (1.0 / 65536.0)
    high_weight, low_weight = jnp.zeros_like(hit), jnp.zeros_like(hit)
    for k in range(picks):
        same = jnp.where(names[:, k : k + 1] == owner, hit, 0.0)
        high_weight = high_weight + same * high[:, k : k + 1]
        low_weight = low_weight + same * low[:, k : k + 1]
        mine_ref[k * tokens : (k + 1) * tokens, :] = same.astype(BF16)
    weight_ref[:tokens, :] = high_weight.astype(BF16)
    weight_ref[tokens:, :] = low_weight.astype(BF16)


def plan(meta, chips, picks):
    tokens = len(meta) * meta[0].shape[0]
    rows = chips * len(meta) * SLOT
    return pl.pallas_call(
        functools.partial(plan_kernel, chips, picks),
        out_shape=(
            jax.ShapeDtypeStruct((2 * tokens, rows), BF16),
            jax.ShapeDtypeStruct((picks * tokens, rows), BF16),
        ),
        in_specs=[VMEM] * len(meta),
        out_specs=(VMEM, VMEM),
        cost_estimate=SMALL,
        compiler_params=pltpu.CompilerParams(vmem_limit_bytes=8 * MIB),
        name="plan_sums",
    )(*meta)


def turn_kernel(keep, weight_hbm, after_ref, *refs):
    held, turned, sems = refs
    step = PIECE
    pieces = weight_hbm.shape[0] // step
    copies = []
    for p in range(pieces):
        cut = pl.ds(p * step, step)
        copies.append(pltpu.make_async_copy(weight_hbm.at[cut], held.at[cut], sems.at[p]))
        copies[-1].start()
    for p in range(pieces):
        copies[p].wait()
        cut = pl.ds(p * step, step)
        turned[:, cut] = jnp.transpose(held[cut, :])


def turn(weight, keep, after):
    rows, cols = weight.shape
    held, turned = pltpu.VMEM((rows, cols), BF16), pltpu.VMEM((cols, rows), BF16)
    return pl.pallas_call(
        functools.partial(turn_kernel, keep),
        out_shape=(held, turned) if keep else (turned,),
        in_specs=[HBM, VMEM],
        out_specs=(VMEM, VMEM) if keep else (VMEM,),
        scratch_shapes=([] if keep else [held]) + [pltpu.SemaphoreType.DMA((rows // PIECE,))],
        cost_estimate=SMALL,
        compiler_params=pltpu.CompilerParams(vmem_limit_bytes=12 * MIB),
        name="turn_weight",
    )(in_hbm(weight), after)


def turn_drop_kernel(weight_hbm, after_ref, turned, held, sems):
    turn_kernel(False, weight_hbm, after_ref, held, turned, sems)


def turn_only(weight, after):
    rows, cols = weight.shape
    return pl.pallas_call(
        turn_drop_kernel,
        out_shape=pltpu.VMEM((cols, rows), BF16),
        in_specs=[HBM, VMEM],
        out_specs=VMEM,
        scratch_shapes=[pltpu.VMEM((rows, cols), BF16), pltpu.SemaphoreType.DMA((rows // PIECE,))],
        cost_estimate=SMALL,
        compiler_params=pltpu.CompilerParams(vmem_limit_bytes=12 * MIB),
        name="turn_weight",
    )(in_hbm(weight), after)


def gather_kernel(count, *refs):
    out_ref = refs[-1]
    lines = refs[0].shape[0]
    for b in range(count):
        out_ref[b * lines : (b + 1) * lines, :] = refs[b][...]


def gather_rows(arrived, after):
    count, (lines, wide) = len(arrived), arrived[0].shape
    return pl.pallas_call(
        functools.partial(gather_kernel, count),
        out_shape=jax.ShapeDtypeStruct((count * lines, wide), BF16),
        in_specs=[VMEM] * (count + len(after)),
        out_specs=VMEM,
        cost_estimate=COST,
        compiler_params=pltpu.CompilerParams(vmem_limit_bytes=4 * MIB),
        name="gather_rows",
    )(*arrived, *after)


def expert_kernel(count, extra, first_ref, *refs):
    arrived, refs = refs[:count], refs[extra:]
    gate_ref, up_ref, gate_t_ref, up_t_ref, down_t_ref = refs[count : count + 5]
    backs = refs[count + 5 : 3 * count + 5]
    rows_ref, gg_ref, gu_ref = refs[3 * count + 5 :]
    width, hidden = gate_ref.shape
    lines = arrived[0].shape[0]
    half = count * lines
    total = 2 * half
    rows_ref[:half, :] = first_ref[...]
    for b in range(count):
        rows_ref[half + b * lines : half + (b + 1) * lines, :] = arrived[b][...]
    tile = math.gcd(hidden, 512)

    def hidden_tile(i, score):
        cols = pl.ds(pl.multiple_of(i * tile, tile), tile)
        rows_in = rows_ref[:, :width]
        pre_gate = jnp.dot(rows_in, gate_ref[:, cols], preferred_element_type=F32)
        pre_up = jnp.dot(rows_in, up_ref[:, cols], preferred_element_type=F32)
        grad_hidden = jnp.dot(rows_ref[:, width:], down_t_ref[:, cols], preferred_element_type=F32)
        sigmoid = 1.0 / (1.0 + jnp.exp(-pre_gate))
        activated = pre_gate * sigmoid
        grad_up = grad_hidden * activated
        gg_ref[:, cols] = (
            grad_hidden * pre_up * sigmoid * (1.0 + pre_gate * (1.0 - sigmoid))
        ).astype(BF16)
        gu_ref[:, cols] = grad_up.astype(BF16)
        return score + jnp.sum(grad_up * pre_up, axis=1, keepdims=True)

    score = lax.fori_loop(0, hidden // tile, hidden_tile, jnp.zeros((total, 1), F32))
    score = jnp.broadcast_to(score, (total, LANES)).astype(BF16)
    for b in range(2 * count):
        backs[b][:, width:] = score[b * lines : (b + 1) * lines, :]
    step = math.gcd(width, 512)

    def row_tile(i, carry):
        cols = pl.ds(pl.multiple_of(i * step, step), step)
        row = jnp.dot(gg_ref[...], gate_t_ref[:, cols], preferred_element_type=F32)
        row = row + jnp.dot(gu_ref[...], up_t_ref[:, cols], preferred_element_type=F32)
        row = row.astype(BF16)
        for b in range(2 * count):
            backs[b][:, cols] = row[b * lines : (b + 1) * lines, :]
        return carry

    lax.fori_loop(0, width // step, row_tile, 0)


def expert(first, arrived, weights, after):
    width, hidden = weights[0].shape
    count, lines = len(arrived), arrived[0].shape[0]
    held = tuple(in_vmem(w) for w in weights)
    rows = 2 * count * lines
    return pl.pallas_call(
        functools.partial(expert_kernel, count, len(after)),
        out_shape=(jax.ShapeDtypeStruct((lines, width + LANES), BF16),) * (2 * count),
        in_specs=[VMEM] * (1 + count + len(after) + len(held)),
        out_specs=(VMEM,) * (2 * count),
        scratch_shapes=[
            pltpu.VMEM((rows, 2 * width), BF16),
            pltpu.VMEM((rows, hidden), BF16),
            pltpu.VMEM((rows, hidden), BF16),
        ],
        cost_estimate=SMALL,
        compiler_params=pltpu.CompilerParams(vmem_limit_bytes=max(8, rows // 20) * MIB),
        name="expert_rows",
    )(first, *arrived, *after, *held)


def combine_kernel(picks, weight_ref, mine_ref, *refs):
    backs, (keep_ref, send_ref) = refs[:-2], refs[-2:]
    lines, wide = backs[0].shape
    width = wide - LANES
    tokens = weight_ref.shape[0] // 2
    own = tokens // 4
    parts = ((keep_ref, 0), (send_ref, own))
    for at in range(0, width, 512):
        step = min(512, width - at)
        rows = jnp.concatenate([b[:, at : at + step] for b in backs], axis=0)
        total = jnp.dot(weight_ref[...], rows, preferred_element_type=F32)
        total = (total[:tokens] + total[tokens:]).astype(BF16)
        for ref, first in parts:
            for z in range(2):
                ref[z * own : (z + 1) * own, at : at + step] = total[
                    first + 2 * z * own : first + (2 * z + 1) * own, :
                ]
    marks = jnp.concatenate([b[:, width:] for b in backs], axis=0)
    value = jnp.dot(mine_ref[...], marks, preferred_element_type=F32)
    lane = iota((tokens, LANES), 1)
    spread = jnp.zeros((tokens, LANES), F32)
    for k in range(picks):
        spread = jnp.where(lane == k, value[k * tokens : (k + 1) * tokens, :], spread)
    spread = spread.astype(BF16)
    for ref, first in parts:
        for z in range(2):
            ref[z * own : (z + 1) * own, width:] = spread[
                first + 2 * z * own : first + (2 * z + 1) * own, :
            ]


def combine(sums, backs, picks):
    tokens = sums[0].shape[0] // 2
    shape = jax.ShapeDtypeStruct((tokens // 2, backs[0].shape[1]), BF16)
    return pl.pallas_call(
        functools.partial(combine_kernel, picks),
        out_shape=(shape, shape),
        in_specs=[VMEM] * (2 + len(backs)),
        out_specs=(VMEM, VMEM),
        cost_estimate=SMALL,
        compiler_params=pltpu.CompilerParams(vmem_limit_bytes=8 * MIB),
        name="combine_rows",
    )(*sums, *backs)


def join_kernel(keep_ref, got_ref, first_ref, second_ref):
    tokens = first_ref.shape[0]
    total = keep_ref[...].astype(F32) + got_ref[...].astype(F32)
    first_ref[...] = total[:tokens, :]
    second_ref[...] = total[tokens:, :].astype(BF16)


def join(keep, got):
    shape = (keep.shape[0] // 2, keep.shape[1])
    return pl.pallas_call(
        join_kernel,
        out_shape=(jax.ShapeDtypeStruct(shape, F32), jax.ShapeDtypeStruct(shape, BF16)),
        in_specs=[VMEM, VMEM],
        out_specs=(VMEM, VMEM),
        cost_estimate=SMALL,
        compiler_params=pltpu.CompilerParams(vmem_limit_bytes=8 * MIB),
        name="join_cores",
    )(keep, got)


def add_kernel(first_ref, got_ref, out_ref):
    out_ref[...] = (first_ref[...] + got_ref[...].astype(F32)).astype(BF16)


def add(first, got):
    return pl.pallas_call(
        add_kernel,
        out_shape=jax.ShapeDtypeStruct(got.shape, BF16),
        in_specs=[VMEM, VMEM],
        out_specs=VMEM,
        cost_estimate=SMALL,
        compiler_params=pltpu.CompilerParams(vmem_limit_bytes=8 * MIB),
        name="add_planes",
    )(first, got)


def finish_kernel(*refs):
    parts, (out_ref, gate_grad_ref) = refs[:-2], refs[-2:]
    tokens, width = out_ref.shape
    picks = gate_grad_ref.shape[0]
    total = parts[0][...].astype(F32)
    for part in parts[1:]:
        total = total + part[...].astype(F32)
    out_ref[...] = total[:, :width].astype(BF16)
    scores = total[:, width : width + picks].astype(BF16)
    gate_grad_ref[...] = lax.dot_general(
        scores, unit(tokens), TN, preferred_element_type=F32
    ).astype(BF16)


def finish(parts, picks):
    tokens, wide = parts[0].shape
    return pl.pallas_call(
        finish_kernel,
        out_shape=(
            jax.ShapeDtypeStruct((tokens, wide - LANES), BF16),
            jax.ShapeDtypeStruct((picks, tokens), BF16),
        ),
        in_specs=[VMEM] * len(parts),
        out_specs=(VMEM, VMEM),
        cost_estimate=SMALL,
        compiler_params=pltpu.CompilerParams(vmem_limit_bytes=8 * MIB),
        name="finish_tokens",
    )(*parts)


def relay_kernel(cuts, array_ref, *refs):
    outs, at = refs[-len(cuts) :], 0
    for cut, out in zip(cuts, outs):
        out[...] = array_ref[:, at : at + cut]
        at += cut


def relay(array, cuts, after):
    rows = array.shape[0]
    return pl.pallas_call(
        functools.partial(relay_kernel, cuts),
        out_shape=tuple(jax.ShapeDtypeStruct((rows, c), array.dtype) for c in cuts),
        in_specs=[VMEM] * (1 + len(after)),
        out_specs=(VMEM,) * len(cuts),
        cost_estimate=SMALL,
        compiler_params=pltpu.CompilerParams(vmem_limit_bytes=4 * MIB),
        name="relay",
    )(array, *(in_vmem(a) for a in after))


def swap(array, axis, mask):
    count = lax.axis_size(axis)
    return lax.ppermute(array, axis, [(i, i ^ mask) for i in range(count)])


def shards(out_grad, saved_input, routes, gate_int, w_gate, w_up, w_down):
    picks = routes.shape[1]
    chips = lax.axis_size("chip")
    width = saved_input.shape[1]
    cuts = (width + LANES, width)
    own = pack(saved_input, out_grad, routes.T, gate_int.T)
    far = swap(own, "far", 1)
    near = swap(own, "near", 1)
    beside = swap(own, "core", 1)
    gate, gate_t = turn(w_gate[0], True, own)
    (near,) = relay(near, (sum(cuts),), (gate_t,))
    here = ((own,), (beside,), (near,), (swap(near, "core", 1),))
    sent = dispatch(here, chips, picks, ())
    here_sums = plan([b[0][:, width : width + LANES] for b in here], chips, picks)
    here_rows = [sent[0]] + [swap(sent[j], "chip", j) for j in range(1, chips)]
    up, up_t = turn(w_up[0], True, sent[0])
    across = relay(swap(far, "near", 1), cuts, (up_t,))
    there = (
        (far,),
        (swap(far, "core", 1),),
        across,
        tuple(swap(a, "core", 1) for a in across),
    )
    sent = dispatch(there, chips, picks, ())
    there_sums = plan([b[0][:, width : width + LANES] for b in there], chips, picks)
    there_rows = [sent[0]] + [swap(sent[j], "chip", j) for j in range(1, chips)]
    down_t = turn_only(w_down[0], sent[0])
    first = gather_rows(here_rows, (there_sums[0], here_sums[0]))
    backs = expert(first, there_rows, (gate, up, gate_t, up_t, down_t), ())
    here_back, there_back = backs[:chips], backs[chips:]

    def gather(back, sums):
        rows = [back[0]] + [swap(back[j], "chip", j) for j in range(1, chips)]
        keep, send = combine(sums, rows, picks)
        return join(keep, swap(send, "core", 1))

    first, second = gather(there_back, there_sums)
    away = swap(add(first, swap(second, "near", 1)), "far", 1)
    first, second = gather(here_back, here_sums)
    parts = (first, swap(second, "near", 1), away)
    input_grad, gate_grad = finish(parts, picks)
    return input_grad, gate_grad.T


def solution(mesh):
    devices = mesh.devices
    split = Mesh(devices.reshape(2, 2, devices.size // 8, 2), AXES)
    rows, stack = P(AXES, None), P(AXES, None, None)
    return jax.shard_map(
        shards,
        mesh=split,
        in_specs=(rows,) * 4 + (stack,) * 3,
        out_specs=(rows, rows),
        check_vma=False,
    )
```

```python
import functools
import math

import jax
import jax.numpy as jnp
from jax import lax
from jax.experimental import pallas as pl
from jax.experimental.pallas import tpu as pltpu
from jax.sharding import Mesh
from jax.sharding import PartitionSpec as P

F32 = jnp.float32
BF16 = jnp.bfloat16
LANES = 128
SLOT = 4
AXES = ("far", "near", "chip", "core")
TN = (((0,), (0,)), ((), ()))
VMEM = pl.BlockSpec(memory_space=pltpu.VMEM)
HBM = pl.BlockSpec(memory_space=pltpu.HBM)
ANY = pl.BlockSpec(memory_space=pl.ANY)
MIB = 2**20
PIECE = 256
SMALL = pl.CostEstimate(flops=1, bytes_accessed=1, transcendentals=0)


def iota(shape, dim):
    return lax.broadcasted_iota(jnp.int32, shape, dim)


def exact(mask):
    return mask.astype(F32).astype(BF16)


def in_hbm(array):
    return pltpu.with_memory_space_constraint(array, pltpu.HBM)


def in_vmem(array):
    return pltpu.with_memory_space_constraint(array, pltpu.VMEM)


def unit(count):
    return exact(iota((count, count), 0) == iota((count, count), 1))


def pack_kernel(input_hbm, grad_hbm, routes_hbm, gate_hbm, out_ref, routes_ref, gate_ref, sems):
    width = input_hbm.shape[1]
    copies = [
        pltpu.make_async_copy(routes_hbm, routes_ref, sems.at[0]),
        pltpu.make_async_copy(gate_hbm, gate_ref, sems.at[1]),
        pltpu.make_async_copy(input_hbm, out_ref.at[:, pl.ds(0, width)], sems.at[2]),
        pltpu.make_async_copy(grad_hbm, out_ref.at[:, pl.ds(width + LANES, width)], sems.at[3]),
    ]
    for copy in copies:
        copy.start()
    copies[0].wait()
    copies[1].wait()
    picks = routes_ref.shape[0]
    gate = gate_ref[...]
    table = jnp.concatenate([routes_ref[...], gate // 256, gate % 256], axis=0)
    place = exact(iota((3 * picks, LANES), 0) == iota((3 * picks, LANES), 1))
    out_ref[:, width : width + LANES] = lax.dot_general(
        table.astype(F32).astype(BF16), place, TN, preferred_element_type=F32
    ).astype(BF16)
    copies[2].wait()
    copies[3].wait()


def pack(input_rows, grad_rows, routes_t, gate_t):
    tokens, width = input_rows.shape
    return pl.pallas_call(
        pack_kernel,
        out_shape=jax.ShapeDtypeStruct((tokens, 2 * width + LANES), BF16),
        in_specs=[HBM] * 4,
        out_specs=VMEM,
        scratch_shapes=[
            pltpu.VMEM(routes_t.shape, jnp.int32),
            pltpu.VMEM(gate_t.shape, jnp.int32),
            pltpu.SemaphoreType.DMA((4,)),
        ],
        cost_estimate=SMALL,
        compiler_params=pltpu.CompilerParams(vmem_limit_bytes=4 * MIB),
        name="pack_tokens",
    )(*(in_hbm(a) for a in (input_rows, grad_rows, routes_t, gate_t)))


def choose(meta, chips, picks):
    tokens = meta[0].shape[0]
    blocks = len(meta)
    lines = blocks * SLOT
    names = jnp.concatenate([m[:, :picks] for m in meta], axis=0).astype(F32)
    shape = (blocks * tokens, chips * lines)
    lane, row = iota(shape, 1), iota(shape, 0)
    chip = jnp.bitwise_xor(lane // lines, lax.axis_index("chip"))
    plane = lax.axis_index("far") * 2 + lax.axis_index("near")
    owner = (2 * (plane * chips + chip) + lax.axis_index("core")).astype(F32)
    named = jnp.zeros(shape, F32)
    for k in range(picks):
        named = named + (names[:, k : k + 1] == owner).astype(F32)
    square = (blocks * tokens, blocks * tokens)
    r, c = iota(square, 0), iota(square, 1)
    before = exact(jnp.logical_and(c < r, c // tokens == r // tokens))
    rank = jnp.dot(before, named.astype(BF16), preferred_element_type=F32)
    fits = jnp.logical_and(rank == (lane % SLOT).astype(F32), (lane // SLOT) % blocks == row // tokens)
    return names, owner, jnp.where(fits, named, 0.0)


def dispatch_kernel(kinds, chips, picks, extra, *refs):
    outs = refs[-chips:]
    width = outs[0].shape[1] // 2
    blocks, at = [], 0
    for kind in kinds:
        if kind == 1:
            blocks.append((refs[at], refs[at], width + LANES))
        else:
            blocks.append((refs[at], refs[at + 1], 0))
        at += kind
    meta = [b[0][:, width : width + LANES] for b in blocks]
    _, _, hit = choose(meta, chips, picks)
    pick = hit.astype(BF16)
    lines = len(blocks) * SLOT
    step = math.gcd(width, 512)
    for part in range(2):
        for at in range(0, width, step):
            rows = jnp.concatenate(
                [
                    grads[:, first + at : first + at + step] if part else ins[:, at : at + step]
                    for ins, grads, first in blocks
                ],
                axis=0,
            )
            moved = lax.dot_general(pick, rows, TN, preferred_element_type=F32)
            for j in range(chips):
                outs[j][:, part * width + at : part * width + at + step] = moved[
                    j * lines : (j + 1) * lines, :
                ].astype(BF16)


def dispatch(blocks, chips, picks, after):
    kinds = tuple(len(b) for b in blocks)
    flat = [a for b in blocks for a in b]
    wide = sum(a.shape[1] for a in blocks[0]) - LANES
    lines = len(blocks) * SLOT
    return pl.pallas_call(
        functools.partial(dispatch_kernel, kinds, chips, picks, len(after)),
        out_shape=(jax.ShapeDtypeStruct((lines, wide), BF16),) * chips,
        in_specs=[VMEM] * (len(flat) + len(after)),
        out_specs=(VMEM,) * chips,
        cost_estimate=SMALL,
        compiler_params=pltpu.CompilerParams(vmem_limit_bytes=8 * MIB),
        name="dispatch_rows",
    )(*flat, *(in_vmem(a) for a in after))


def plan_kernel(chips, picks, *refs):
    meta, (weight_ref, mine_ref) = refs[:-2], refs[-2:]
    names, owner, hit = choose([m[...] for m in meta], chips, picks)
    tokens = names.shape[0]
    bytes_of = lambda part: jnp.concatenate(
        [m[:, part * picks : (part + 1) * picks] for m in meta], axis=0
    ).astype(F32)
    high, low = bytes_of(1) * (1.0 / 256.0), bytes_of(2) * (1.0 / 65536.0)
    high_weight, low_weight = jnp.zeros_like(hit), jnp.zeros_like(hit)
    for k in range(picks):
        same = jnp.where(names[:, k : k + 1] == owner, hit, 0.0)
        high_weight = high_weight + same * high[:, k : k + 1]
        low_weight = low_weight + same * low[:, k : k + 1]
        mine_ref[k * tokens : (k + 1) * tokens, :] = same.astype(BF16)
    weight_ref[:tokens, :] = high_weight.astype(BF16)
    weight_ref[tokens:, :] = low_weight.astype(BF16)


def plan(meta, chips, picks):
    tokens = len(meta) * meta[0].shape[0]
    rows = chips * len(meta) * SLOT
    return pl.pallas_call(
        functools.partial(plan_kernel, chips, picks),
        out_shape=(
            jax.ShapeDtypeStruct((2 * tokens, rows), BF16),
            jax.ShapeDtypeStruct((picks * tokens, rows), BF16),
        ),
        in_specs=[VMEM] * len(meta),
        out_specs=(VMEM, VMEM),
        cost_estimate=SMALL,
        compiler_params=pltpu.CompilerParams(vmem_limit_bytes=8 * MIB),
        name="plan_sums",
    )(*meta)


def turn_kernel(count, *refs):
    weights, sems = refs[:count], refs[-1]
    helds, turneds = refs[-1 - 2 * count : -1 - count], refs[-1 - count : -1]
    copies = []
    for w, (weight, held, turned) in enumerate(zip(weights, helds, turneds)):
        for p in range(weight.shape[0] // PIECE):
            cut = pl.ds(p * PIECE, PIECE)
            copy = pltpu.make_async_copy(weight.at[cut], held.at[cut], sems.at[w, p])
            copy.start()
            copies.append((copy, cut, held, turned))
    for copy, cut, held, turned in copies:
        copy.wait()
        turned[:, cut] = jnp.transpose(held[cut, :])


def turn(weights, after):
    rows, cols = weights[0].shape
    count = len(weights)
    return pl.pallas_call(
        functools.partial(turn_kernel, count),
        out_shape=(pltpu.VMEM((rows, cols), BF16),) * count + (pltpu.VMEM((cols, rows), BF16),) * count,
        in_specs=[HBM] * count + [VMEM],
        out_specs=(VMEM,) * (2 * count),
        scratch_shapes=[pltpu.SemaphoreType.DMA((count, rows // PIECE))],
        cost_estimate=SMALL,
        compiler_params=pltpu.CompilerParams(vmem_limit_bytes=4 * MIB),
        name="turn_weights",
    )(*(in_hbm(w) for w in weights), after)


def turn_only_kernel(weight_hbm, after_ref, turned, held, sems):
    turn_kernel(1, weight_hbm, held, turned, sems)


def turn_only(weight, after):
    rows, cols = weight.shape
    return pl.pallas_call(
        turn_only_kernel,
        out_shape=pltpu.VMEM((cols, rows), BF16),
        in_specs=[HBM, VMEM],
        out_specs=VMEM,
        scratch_shapes=[pltpu.VMEM((rows, cols), BF16), pltpu.SemaphoreType.DMA((1, rows // PIECE))],
        cost_estimate=SMALL,
        compiler_params=pltpu.CompilerParams(vmem_limit_bytes=12 * MIB),
        name="turn_weight",
    )(in_hbm(weight), after)


def stack(refs, cut):
    return jnp.concatenate([r[:, cut].astype(F32) for r in refs], axis=0).astype(BF16)


def gather_kernel(count, extra, *refs):
    out_ref = refs[-1]
    wide = out_ref.shape[1]
    step = math.gcd(wide, 1024)
    for at in range(0, wide, step):
        out_ref[:, at : at + step] = stack(refs[:count], slice(at, at + step))


def gather_rows(arrays, after):
    count, (each, wide) = len(arrays), arrays[0].shape
    return pl.pallas_call(
        functools.partial(gather_kernel, count, len(after)),
        out_shape=jax.ShapeDtypeStruct((count * each, wide), BF16),
        in_specs=[VMEM] * (count + len(after)),
        out_specs=VMEM,
        cost_estimate=SMALL,
        compiler_params=pltpu.CompilerParams(vmem_limit_bytes=8 * MIB),
        name="gather_rows",
    )(*arrays, *after)


def by_chip(values, b, count):
    each = values.shape[0] // (4 * count)
    starts = (2 * each * b, 2 * each * count + each * b, 3 * each * count + each * b)
    return jnp.concatenate(
        [values[at : at + n] for at, n in zip(starts, (2 * each, each, each))], axis=0
    ).astype(BF16)


def row_tiles(gg_ref, gu_ref, gate_t_ref, up_t_ref, first, backs, width):
    for at in range(0, width, 512):
        step = min(512, width - at)
        cols = slice(first + at, first + at + step)
        row = jnp.dot(gg_ref[...], gate_t_ref[:, cols], preferred_element_type=F32)
        row = row + jnp.dot(gu_ref[...], up_t_ref[:, cols], preferred_element_type=F32)
        for b, back in enumerate(backs):
            back[:, at : at + step] = by_chip(row, b, len(backs))


def expert_kernel(count, middle_ref, first_ref, *refs):
    arrived, refs = refs[:count], refs[count:]
    gate_ref, up_ref, gate_t_ref, up_t_ref, down_t_ref = refs[:5]
    backs = refs[5 : 5 + count]
    gg_ref, gu_ref, rows_ref = refs[5 + count :]
    width, hidden = gate_ref.shape
    half, total = middle_ref.shape[0], 2 * middle_ref.shape[0]
    early = half + first_ref.shape[0]
    rows_ref[:half, :] = middle_ref[...]
    rows_ref[half:early, :] = first_ref[...]
    for at in range(0, 2 * width, 512):
        cut = slice(at, at + 512)
        rows_ref[early:, cut] = stack(arrived, cut)
    tile = math.gcd(hidden, 512)

    def hidden_tile(i, score):
        cols = pl.ds(pl.multiple_of(i * tile, tile), tile)
        rows_in = rows_ref[:, :width]
        pre_gate = jnp.dot(rows_in, gate_ref[:, cols], preferred_element_type=F32)
        pre_up = jnp.dot(rows_in, up_ref[:, cols], preferred_element_type=F32)
        grad_hidden = jnp.dot(rows_ref[:, width:], down_t_ref[:, cols], preferred_element_type=F32)
        sigmoid = 1.0 / (1.0 + jnp.exp(-pre_gate))
        activated = pre_gate * sigmoid
        grad_up = grad_hidden * activated
        gg_ref[:, cols] = (
            grad_hidden * pre_up * sigmoid * (1.0 + pre_gate * (1.0 - sigmoid))
        ).astype(BF16)
        gu_ref[:, cols] = grad_up.astype(BF16)
        return score + jnp.sum(grad_up * pre_up, axis=1, keepdims=True)

    score = lax.fori_loop(0, hidden // tile, hidden_tile, jnp.zeros((total, 1), F32))
    score = jnp.broadcast_to(score, (total, LANES))
    cols = backs[0].shape[1] - LANES
    for b, back in enumerate(backs):
        back[:, cols:] = by_chip(score, b, count)
    row_tiles(gg_ref, gu_ref, gate_t_ref, up_t_ref, 0, backs, cols)


def expert(middle, first, arrived, weights, cols):
    width, hidden = weights[0].shape
    count, lines = len(arrived), 2 * arrived[0].shape[0]
    held = tuple(in_vmem(w) for w in weights)
    rows = 2 * count * lines
    part = jax.ShapeDtypeStruct((rows, hidden), BF16)
    outs = pl.pallas_call(
        functools.partial(expert_kernel, count),
        out_shape=(jax.ShapeDtypeStruct((2 * lines, cols + LANES), BF16),) * count + (part, part),
        in_specs=[VMEM] * (2 + count + len(held)),
        out_specs=(VMEM,) * (count + 2),
        scratch_shapes=[pltpu.VMEM((rows, 2 * width), BF16)],
        cost_estimate=SMALL,
        compiler_params=pltpu.CompilerParams(vmem_limit_bytes=max(8, rows // 20) * MIB),
        name="expert_rows",
    )(middle, first, *arrived, *held)
    return outs[:count], outs[count:]


def expert_rest_kernel(first, gg_ref, gu_ref, gate_t_ref, up_t_ref, *backs):
    row_tiles(gg_ref, gu_ref, gate_t_ref, up_t_ref, first, backs, backs[0].shape[1])


def expert_rest(part, gate_t, up_t, cols, count):
    lines = part[0].shape[0] // count
    return pl.pallas_call(
        functools.partial(expert_rest_kernel, cols),
        out_shape=(jax.ShapeDtypeStruct((lines, gate_t.shape[1] - cols), BF16),) * count,
        in_specs=[VMEM] * 4,
        out_specs=(VMEM,) * count,
        cost_estimate=SMALL,
        compiler_params=pltpu.CompilerParams(vmem_limit_bytes=8 * MIB),
        name="expert_rest",
    )(*part, in_vmem(gate_t), in_vmem(up_t))


def combine_kernel(picks, marked, *refs):
    weights, mines, refs = refs[:2], refs[2:4], refs[4:]
    backs, (keep_ref, send_ref) = refs[:-2], refs[-2:]
    lines, wide = backs[0].shape
    lines = lines // 2
    width = wide - LANES if marked else wide
    tokens = weights[0].shape[0] // 2
    own = tokens // 4

    def put(batch, values, cols):
        for z in range(2):
            at = (2 * batch + z) * own
            for side, ref in enumerate((keep_ref, send_ref)):
                first = (2 * z + side) * own
                ref[at : at + own, cols] = values[first : first + own, :]

    for batch in range(2):
        cut = slice(batch * lines, (batch + 1) * lines)
        for at in range(0, width, 512):
            cols = slice(at, min(at + 512, width))
            rows = jnp.concatenate([b[cut, cols] for b in backs], axis=0)
            total = jnp.dot(weights[batch][...], rows, preferred_element_type=F32)
            put(batch, (total[:tokens] + total[tokens:]).astype(BF16), cols)
        if marked:
            marks = jnp.concatenate([b[cut, width:] for b in backs], axis=0)
            value = jnp.dot(mines[batch][...], marks, preferred_element_type=F32)
            lane = iota((tokens, LANES), 1)
            spread = jnp.zeros((tokens, LANES), F32)
            for k in range(picks):
                spread = jnp.where(lane == k, value[k * tokens : (k + 1) * tokens, :], spread)
            put(batch, spread.astype(BF16), slice(width, wide))


def combine(sums, backs, picks, marked):
    tokens = sums[0][0].shape[0] // 2
    shape = jax.ShapeDtypeStruct((tokens, backs[0].shape[1]), BF16)
    return pl.pallas_call(
        functools.partial(combine_kernel, picks, marked),
        out_shape=(shape, shape),
        in_specs=[VMEM] * (4 + len(backs)),
        out_specs=(VMEM, VMEM),
        cost_estimate=SMALL,
        compiler_params=pltpu.CompilerParams(vmem_limit_bytes=8 * MIB),
        name="combine_rows",
    )(sums[0][0], sums[1][0], sums[0][1], sums[1][1], *backs)


def join_kernel(keep_ref, got_ref, *outs):
    tokens = outs[0].shape[0]
    total = keep_ref[...].astype(F32) + got_ref[...].astype(F32)
    for z, out in enumerate(outs):
        out[...] = total[z * tokens : (z + 1) * tokens, :].astype(out.dtype)


def join(keep, got):
    shape = (keep.shape[0] // 4, keep.shape[1])
    return pl.pallas_call(
        join_kernel,
        out_shape=tuple(jax.ShapeDtypeStruct(shape, t) for t in (BF16, BF16, F32, BF16)),
        in_specs=[VMEM, VMEM],
        out_specs=(VMEM,) * 4,
        cost_estimate=SMALL,
        compiler_params=pltpu.CompilerParams(vmem_limit_bytes=8 * MIB),
        name="join_cores",
    )(keep, got)


def finish_kernel(picks, *refs):
    parts, (out_ref, gate_grad_ref) = refs[:-2], refs[-2:]
    tokens, width = out_ref.shape
    at = 0
    for p in range(0, len(parts), 4):
        total = parts[p][...]
        for part in parts[p + 1 : p + 4]:
            total = total + part[...].astype(F32)
        cols = total.shape[1] - (0 if p else LANES)
        out_ref[:, at : at + cols] = total[:, :cols].astype(BF16)
        at += cols
        if not p:
            scores = total[:, cols : cols + picks].astype(BF16)
            gate_grad_ref[...] = lax.dot_general(
                scores, unit(tokens), TN, preferred_element_type=F32
            ).astype(BF16)


def finish(parts, width, picks):
    tokens = parts[0].shape[0]
    return pl.pallas_call(
        functools.partial(finish_kernel, picks),
        out_shape=(
            jax.ShapeDtypeStruct((tokens, width), BF16),
            jax.ShapeDtypeStruct((picks, tokens), BF16),
        ),
        in_specs=[VMEM] * len(parts),
        out_specs=(VMEM, VMEM),
        cost_estimate=SMALL,
        compiler_params=pltpu.CompilerParams(vmem_limit_bytes=8 * MIB),
        name="finish_tokens",
    )(*parts)


def relay_kernel(cuts, array_ref, *refs):
    outs, at = refs[-len(cuts) :], 0
    for cut, out in zip(cuts, outs):
        out[...] = array_ref[:, at : at + cut]
        at += cut


def relay(array, cuts, after):
    rows = array.shape[0]
    return pl.pallas_call(
        functools.partial(relay_kernel, cuts),
        out_shape=tuple(jax.ShapeDtypeStruct((rows, c), array.dtype) for c in cuts),
        in_specs=[VMEM] * (1 + len(after)),
        out_specs=(VMEM,) * len(cuts),
        cost_estimate=SMALL,
        compiler_params=pltpu.CompilerParams(vmem_limit_bytes=4 * MIB),
        name="relay",
    )(array, *(in_vmem(a) for a in after))


def swap(array, axis, mask):
    count = lax.axis_size(axis)
    return lax.ppermute(array, axis, [(i, i ^ mask) for i in range(count)])


def shards(out_grad, saved_input, routes, gate_int, w_gate, w_up, w_down):
    picks = routes.shape[1]
    chips = lax.axis_size("chip")
    width = saved_input.shape[1]
    cuts = (width + LANES, width)
    own = pack(saved_input, out_grad, routes.T, gate_int.T)
    far = swap(own, "far", 1)
    near = swap(own, "near", 1)
    beside = swap(own, "core", 1)
    def spread(blocks, after):
        sent = dispatch(blocks, chips, picks, after)
        return [sent[0]] + [swap(sent[j], "chip", j) for j in range(1, chips)]

    pair = ((own,), (beside,))
    first_rows = spread(pair, ())
    gate, up, gate_t, up_t = turn((w_gate[0], w_up[0]), first_rows[0])
    first = gather_rows(first_rows, ())
    (near,) = relay(near, (sum(cuts),), (gate_t, first))
    (far,) = relay(far, (sum(cuts),), (gate_t,))
    middle_pair = ((near,), (swap(near, "core", 1),), (far,), (swap(far, "core", 1),))
    across = relay(swap(far, "near", 1), cuts, ())
    across_pair = (across, tuple(swap(a, "core", 1) for a in across))
    middle_rows = spread(middle_pair, ())
    sent = list(dispatch(across_pair, chips, picks, ()))
    sums_of = lambda blocks: plan([b[0][:, width : width + LANES] for b in blocks], chips, picks)
    middle_sums, outer_sums = sums_of(middle_pair), sums_of(pair + across_pair)
    middle = gather_rows(middle_rows, (middle_sums[0], outer_sums[0]))
    (sent[-1],) = relay(sent[-1], (2 * width,), (middle,))
    last_rows = [sent[0]] + [swap(sent[j], "chip", j) for j in range(1, chips)]
    down_t = turn_only(w_down[0], last_rows[0])
    weights = (gate, up, gate_t, up_t, down_t)
    cols = width // 2 // LANES * LANES - LANES
    early, part = expert(middle, first, last_rows, weights, cols)
    late = expert_rest(part, gate_t, up_t, cols, chips)
    parts = []
    for back in (early, late):
        rows = [back[0]] + [swap(back[j], "chip", j) for j in range(1, chips)]
        keep, send = combine((middle_sums, outer_sums), rows, picks, back is early)
        near, far, home, across = join(keep, swap(send, "core", 1))
        parts += [home, swap(far, "far", 1), swap(across, ("far", "near"), 3), swap(near, "near", 1)]
    input_grad, gate_grad = finish(parts, width, picks)
    return input_grad, gate_grad.T


def solution(mesh):
    devices = mesh.devices
    split = Mesh(devices.reshape(2, 2, devices.size // 8, 2), AXES)
    rows, stack = P(AXES, None), P(AXES, None, None)
    return jax.shard_map(
        shards,
        mesh=split,
        in_specs=(rows,) * 4 + (stack,) * 3,
        out_specs=(rows, rows),
        check_vma=False,
    )
```

```python
import functools
import math

import jax
import jax.numpy as jnp
from jax import lax
from jax.experimental import pallas as pl
from jax.experimental.pallas import tpu as pltpu
from jax.sharding import Mesh
from jax.sharding import PartitionSpec as P

F32 = jnp.float32
BF16 = jnp.bfloat16
LANES = 128
SLOT = 4
AXES = ("far", "near", "chip", "core")
TN = (((0,), (0,)), ((), ()))
VMEM = pl.BlockSpec(memory_space=pltpu.VMEM)
HBM = pl.BlockSpec(memory_space=pltpu.HBM)
ANY = pl.BlockSpec(memory_space=pl.ANY)
MIB = 2**20
PIECE = 256
SMALL = pl.CostEstimate(flops=1, bytes_accessed=1, transcendentals=0)


def iota(shape, dim):
    return lax.broadcasted_iota(jnp.int32, shape, dim)


def exact(mask):
    return mask.astype(F32).astype(BF16)


def in_hbm(array):
    return pltpu.with_memory_space_constraint(array, pltpu.HBM)


def in_vmem(array):
    return pltpu.with_memory_space_constraint(array, pltpu.VMEM)


def unit(count):
    return exact(iota((count, count), 0) == iota((count, count), 1))


def pack_kernel(input_hbm, grad_hbm, routes_hbm, gate_hbm, out_ref, routes_ref, gate_ref, sems):
    width = input_hbm.shape[1]
    copies = [
        pltpu.make_async_copy(routes_hbm, routes_ref, sems.at[0]),
        pltpu.make_async_copy(gate_hbm, gate_ref, sems.at[1]),
        pltpu.make_async_copy(input_hbm, out_ref.at[:, pl.ds(0, width)], sems.at[2]),
        pltpu.make_async_copy(grad_hbm, out_ref.at[:, pl.ds(width + LANES, width)], sems.at[3]),
    ]
    for copy in copies:
        copy.start()
    copies[0].wait()
    copies[1].wait()
    picks = routes_ref.shape[0]
    gate = gate_ref[...]
    table = jnp.concatenate([routes_ref[...], gate // 256, gate % 256], axis=0)
    place = exact(iota((3 * picks, LANES), 0) == iota((3 * picks, LANES), 1))
    out_ref[:, width : width + LANES] = lax.dot_general(
        table.astype(F32).astype(BF16), place, TN, preferred_element_type=F32
    ).astype(BF16)
    copies[2].wait()
    copies[3].wait()


def pack(input_rows, grad_rows, routes_t, gate_t):
    tokens, width = input_rows.shape
    return pl.pallas_call(
        pack_kernel,
        out_shape=jax.ShapeDtypeStruct((tokens, 2 * width + LANES), BF16),
        in_specs=[HBM] * 4,
        out_specs=VMEM,
        scratch_shapes=[
            pltpu.VMEM(routes_t.shape, jnp.int32),
            pltpu.VMEM(gate_t.shape, jnp.int32),
            pltpu.SemaphoreType.DMA((4,)),
        ],
        cost_estimate=SMALL,
        compiler_params=pltpu.CompilerParams(vmem_limit_bytes=4 * MIB),
        name="pack_tokens",
    )(*(in_hbm(a) for a in (input_rows, grad_rows, routes_t, gate_t)))


def choose(meta, chips, picks):
    tokens = meta[0].shape[0]
    blocks = len(meta)
    lines = blocks * SLOT
    names = jnp.concatenate([m[:, :picks] for m in meta], axis=0).astype(F32)
    shape = (blocks * tokens, chips * lines)
    lane, row = iota(shape, 1), iota(shape, 0)
    chip = jnp.bitwise_xor(lane // lines, lax.axis_index("chip"))
    plane = lax.axis_index("far") * 2 + lax.axis_index("near")
    owner = (2 * (plane * chips + chip) + lax.axis_index("core")).astype(F32)
    named = jnp.zeros(shape, F32)
    for k in range(picks):
        named = named + (names[:, k : k + 1] == owner).astype(F32)
    square = (blocks * tokens, blocks * tokens)
    r, c = iota(square, 0), iota(square, 1)
    before = exact(jnp.logical_and(c < r, c // tokens == r // tokens))
    rank = jnp.dot(before, named.astype(BF16), preferred_element_type=F32)
    fits = jnp.logical_and(rank == (lane % SLOT).astype(F32), (lane // SLOT) % blocks == row // tokens)
    return names, owner, jnp.where(fits, named, 0.0)


def dispatch_kernel(kinds, chips, picks, extra, *refs):
    outs = refs[-chips:]
    width = outs[0].shape[1] // 2
    blocks, at = [], 0
    for kind in kinds:
        if kind == 1:
            blocks.append((refs[at], refs[at], width + LANES))
        else:
            blocks.append((refs[at], refs[at + 1], 0))
        at += kind
    meta = [b[0][:, width : width + LANES] for b in blocks]
    _, _, hit = choose(meta, chips, picks)
    pick = hit.astype(BF16)
    lines = len(blocks) * SLOT
    step = math.gcd(width, 512)
    for part in range(2):
        for at in range(0, width, step):
            rows = jnp.concatenate(
                [
                    grads[:, first + at : first + at + step] if part else ins[:, at : at + step]
                    for ins, grads, first in blocks
                ],
                axis=0,
            )
            moved = lax.dot_general(pick, rows, TN, preferred_element_type=F32)
            for j in range(chips):
                outs[j][:, part * width + at : part * width + at + step] = moved[
                    j * lines : (j + 1) * lines, :
                ].astype(BF16)


def dispatch(blocks, chips, picks, after):
    kinds = tuple(len(b) for b in blocks)
    flat = [a for b in blocks for a in b]
    wide = sum(a.shape[1] for a in blocks[0]) - LANES
    lines = len(blocks) * SLOT
    return pl.pallas_call(
        functools.partial(dispatch_kernel, kinds, chips, picks, len(after)),
        out_shape=(jax.ShapeDtypeStruct((lines, wide), BF16),) * chips,
        in_specs=[VMEM] * (len(flat) + len(after)),
        out_specs=(VMEM,) * chips,
        cost_estimate=SMALL,
        compiler_params=pltpu.CompilerParams(vmem_limit_bytes=8 * MIB),
        name="dispatch_rows",
    )(*flat, *(in_vmem(a) for a in after))


def plan_kernel(chips, picks, *refs):
    meta, (weight_ref, mine_ref) = refs[:-2], refs[-2:]
    names, owner, hit = choose([m[...] for m in meta], chips, picks)
    tokens = names.shape[0]
    bytes_of = lambda part: jnp.concatenate(
        [m[:, part * picks : (part + 1) * picks] for m in meta], axis=0
    ).astype(F32)
    high, low = bytes_of(1) * (1.0 / 256.0), bytes_of(2) * (1.0 / 65536.0)
    high_weight, low_weight = jnp.zeros_like(hit), jnp.zeros_like(hit)
    for k in range(picks):
        same = jnp.where(names[:, k : k + 1] == owner, hit, 0.0)
        high_weight = high_weight + same * high[:, k : k + 1]
        low_weight = low_weight + same * low[:, k : k + 1]
        mine_ref[k * tokens : (k + 1) * tokens, :] = same.astype(BF16)
    weight_ref[:tokens, :] = high_weight.astype(BF16)
    weight_ref[tokens:, :] = low_weight.astype(BF16)


def plan(meta, chips, picks):
    tokens = len(meta) * meta[0].shape[0]
    rows = chips * len(meta) * SLOT
    return pl.pallas_call(
        functools.partial(plan_kernel, chips, picks),
        out_shape=(
            jax.ShapeDtypeStruct((2 * tokens, rows), BF16),
            jax.ShapeDtypeStruct((picks * tokens, rows), BF16),
        ),
        in_specs=[VMEM] * len(meta),
        out_specs=(VMEM, VMEM),
        cost_estimate=SMALL,
        compiler_params=pltpu.CompilerParams(vmem_limit_bytes=8 * MIB),
        name="plan_sums",
    )(*meta)


def turn_kernel(count, *refs):
    weights, sems = refs[:count], refs[-1]
    helds, turneds = refs[-1 - 2 * count : -1 - count], refs[-1 - count : -1]
    copies = []
    for w, (weight, held, turned) in enumerate(zip(weights, helds, turneds)):
        for p in range(weight.shape[0] // PIECE):
            cut = pl.ds(p * PIECE, PIECE)
            copy = pltpu.make_async_copy(weight.at[cut], held.at[cut], sems.at[w, p])
            copy.start()
            copies.append((copy, cut, held, turned))
    for copy, cut, held, turned in copies:
        copy.wait()
        turned[:, cut] = jnp.transpose(held[cut, :])


def turn(weights, after):
    rows, cols = weights[0].shape
    count = len(weights)
    return pl.pallas_call(
        functools.partial(turn_kernel, count),
        out_shape=(pltpu.VMEM((rows, cols), BF16),) * count + (pltpu.VMEM((cols, rows), BF16),) * count,
        in_specs=[HBM] * count + [VMEM],
        out_specs=(VMEM,) * (2 * count),
        scratch_shapes=[pltpu.SemaphoreType.DMA((count, rows // PIECE))],
        cost_estimate=SMALL,
        compiler_params=pltpu.CompilerParams(vmem_limit_bytes=4 * MIB),
        name="turn_weights",
    )(*(in_hbm(w) for w in weights), after)


def turn_only_kernel(weight_hbm, after_ref, turned, held, sems):
    turn_kernel(1, weight_hbm, held, turned, sems)


def turn_only(weight, after):
    rows, cols = weight.shape
    return pl.pallas_call(
        turn_only_kernel,
        out_shape=pltpu.VMEM((cols, rows), BF16),
        in_specs=[HBM, VMEM],
        out_specs=VMEM,
        scratch_shapes=[pltpu.VMEM((rows, cols), BF16), pltpu.SemaphoreType.DMA((1, rows // PIECE))],
        cost_estimate=SMALL,
        compiler_params=pltpu.CompilerParams(vmem_limit_bytes=12 * MIB),
        name="turn_weight",
    )(in_hbm(weight), after)


def stack(refs, cut):
    return jnp.concatenate([r[:, cut].astype(F32) for r in refs], axis=0).astype(BF16)


def gather_kernel(count, extra, *refs):
    out_ref = refs[-1]
    wide = out_ref.shape[1]
    step = math.gcd(wide, 1024)
    for at in range(0, wide, step):
        out_ref[:, at : at + step] = stack(refs[:count], slice(at, at + step))


def gather_rows(arrays, after):
    count, (each, wide) = len(arrays), arrays[0].shape
    return pl.pallas_call(
        functools.partial(gather_kernel, count, len(after)),
        out_shape=jax.ShapeDtypeStruct((count * each, wide), BF16),
        in_specs=[VMEM] * (count + len(after)),
        out_specs=VMEM,
        cost_estimate=SMALL,
        compiler_params=pltpu.CompilerParams(vmem_limit_bytes=8 * MIB),
        name="gather_rows",
    )(*arrays, *after)


def by_chip(values, b, count):
    each = values.shape[0] // (4 * count)
    starts = (2 * each * b, 2 * each * count + each * b, 3 * each * count + each * b)
    return jnp.concatenate(
        [values[at : at + n] for at, n in zip(starts, (2 * each, each, each))], axis=0
    ).astype(BF16)


def row_tiles(gg_ref, gu_ref, gate_t_ref, up_t_ref, first, backs, width):
    for at in range(0, width, 512):
        step = min(512, width - at)
        cols = slice(first + at, first + at + step)
        row = jnp.dot(gg_ref[...], gate_t_ref[:, cols], preferred_element_type=F32)
        row = row + jnp.dot(gu_ref[...], up_t_ref[:, cols], preferred_element_type=F32)
        for b, back in enumerate(backs):
            back[:, at : at + step] = by_chip(row, b, len(backs))


def expert_kernel(count, middle_ref, first_ref, *refs):
    arrived, refs = refs[:count], refs[count:]
    gate_ref, up_ref, gate_t_ref, up_t_ref, down_t_ref = refs[:5]
    backs = refs[5 : 5 + count]
    gg_ref, gu_ref, rows_ref = refs[5 + count :]
    width, hidden = gate_ref.shape
    half, total = middle_ref.shape[0], 2 * middle_ref.shape[0]
    early = half + first_ref.shape[0]
    rows_ref[:half, :] = middle_ref[...]
    rows_ref[half:early, :] = first_ref[...]
    for at in range(0, 2 * width, 512):
        cut = slice(at, at + 512)
        rows_ref[early:, cut] = stack(arrived, cut)
    score = jnp.zeros((total, 1), F32)
    for at in range(0, hidden, 512):
        cols = slice(at, min(at + 512, hidden))
        rows_in = rows_ref[:, :width]
        pre_gate = jnp.dot(rows_in, gate_ref[:, cols], preferred_element_type=F32)
        pre_up = jnp.dot(rows_in, up_ref[:, cols], preferred_element_type=F32)
        grad_hidden = jnp.dot(rows_ref[:, width:], down_t_ref[:, cols], preferred_element_type=F32)
        sigmoid = 1.0 / (1.0 + jnp.exp(-pre_gate))
        activated = pre_gate * sigmoid
        grad_up = grad_hidden * activated
        gg_ref[:, cols] = (
            grad_hidden * pre_up * sigmoid * (1.0 + pre_gate * (1.0 - sigmoid))
        ).astype(BF16)
        gu_ref[:, cols] = grad_up.astype(BF16)
        score = score + jnp.sum(grad_up * pre_up, axis=1, keepdims=True)
    score = jnp.broadcast_to(score, (total, LANES))
    cols = backs[0].shape[1] - LANES
    for b, back in enumerate(backs):
        back[:, cols:] = by_chip(score, b, count)
    row_tiles(gg_ref, gu_ref, gate_t_ref, up_t_ref, 0, backs, cols)


def expert(middle, first, arrived, weights, cols):
    width, hidden = weights[0].shape
    count, lines = len(arrived), 2 * arrived[0].shape[0]
    held = tuple(in_vmem(w) for w in weights)
    rows = 2 * count * lines
    part = jax.ShapeDtypeStruct((rows, hidden), BF16)
    outs = pl.pallas_call(
        functools.partial(expert_kernel, count),
        out_shape=(jax.ShapeDtypeStruct((2 * lines, cols + LANES), BF16),) * count + (part, part),
        in_specs=[VMEM] * (2 + count + len(held)),
        out_specs=(VMEM,) * (count + 2),
        scratch_shapes=[pltpu.VMEM((rows, 2 * width), BF16)],
        cost_estimate=SMALL,
        compiler_params=pltpu.CompilerParams(vmem_limit_bytes=max(8, rows // 20) * MIB),
        name="expert_rows",
    )(middle, first, *arrived, *held)
    return outs[:count], outs[count:]


def expert_rest_kernel(first, gg_ref, gu_ref, gate_t_ref, up_t_ref, *backs):
    row_tiles(gg_ref, gu_ref, gate_t_ref, up_t_ref, first, backs, backs[0].shape[1])


def expert_rest(part, gate_t, up_t, cols, count):
    lines = part[0].shape[0] // count
    return pl.pallas_call(
        functools.partial(expert_rest_kernel, cols),
        out_shape=(jax.ShapeDtypeStruct((lines, gate_t.shape[1] - cols), BF16),) * count,
        in_specs=[VMEM] * 4,
        out_specs=(VMEM,) * count,
        cost_estimate=SMALL,
        compiler_params=pltpu.CompilerParams(vmem_limit_bytes=8 * MIB),
        name="expert_rest",
    )(*part, in_vmem(gate_t), in_vmem(up_t))


def combine_kernel(picks, marked, *refs):
    weights, mines, refs = refs[:2], refs[2:4], refs[4:]
    backs, (keep_ref, send_ref) = refs[:-2], refs[-2:]
    lines, wide = backs[0].shape
    lines = lines // 2
    width = wide - LANES if marked else wide
    tokens = weights[0].shape[0] // 2
    own = tokens // 4

    def put(batch, values, cols):
        for z in range(2):
            at = (2 * batch + z) * own
            for side, ref in enumerate((keep_ref, send_ref)):
                first = (2 * z + side) * own
                ref[at : at + own, cols] = values[first : first + own, :]

    for batch in range(2):
        cut = slice(batch * lines, (batch + 1) * lines)
        for at in range(0, width, 512):
            cols = slice(at, min(at + 512, width))
            rows = jnp.concatenate([b[cut, cols] for b in backs], axis=0)
            total = jnp.dot(weights[batch][...], rows, preferred_element_type=F32)
            put(batch, (total[:tokens] + total[tokens:]).astype(BF16), cols)
        if marked:
            marks = jnp.concatenate([b[cut, width:] for b in backs], axis=0)
            value = jnp.dot(mines[batch][...], marks, preferred_element_type=F32)
            lane = iota((tokens, LANES), 1)
            spread = jnp.zeros((tokens, LANES), F32)
            for k in range(picks):
                spread = jnp.where(lane == k, value[k * tokens : (k + 1) * tokens, :], spread)
            put(batch, spread.astype(BF16), slice(width, wide))


def combine(sums, backs, picks, marked):
    tokens = sums[0][0].shape[0] // 2
    shape = jax.ShapeDtypeStruct((tokens, backs[0].shape[1]), BF16)
    return pl.pallas_call(
        functools.partial(combine_kernel, picks, marked),
        out_shape=(shape, shape),
        in_specs=[VMEM] * (4 + len(backs)),
        out_specs=(VMEM, VMEM),
        cost_estimate=SMALL,
        compiler_params=pltpu.CompilerParams(vmem_limit_bytes=8 * MIB),
        name="combine_rows",
    )(sums[0][0], sums[1][0], sums[0][1], sums[1][1], *backs)


def join_kernel(keep_ref, got_ref, *outs):
    tokens = outs[0].shape[0]
    total = keep_ref[...].astype(F32) + got_ref[...].astype(F32)
    for z, out in enumerate(outs):
        out[...] = total[z * tokens : (z + 1) * tokens, :].astype(out.dtype)


def join_pass_kernel(keep_ref, got_ref, near_ref, far_ref, home_ref):
    tokens = home_ref.shape[0]
    total = keep_ref[...].astype(F32) + got_ref[...].astype(F32)
    near_ref[:tokens, :] = total[:tokens, :].astype(BF16)
    far_ref[...] = total[tokens : 2 * tokens, :]
    home_ref[...] = total[2 * tokens : 3 * tokens, :]
    near_ref[tokens:, :] = total[3 * tokens :, :].astype(BF16)


def join(keep, got, onward):
    tokens, cols = keep.shape[0] // 4, keep.shape[1]
    part = jax.ShapeDtypeStruct((tokens, cols), F32)
    send = jax.ShapeDtypeStruct((tokens, cols), BF16)
    both = jax.ShapeDtypeStruct((2 * tokens, cols), BF16)
    shapes = (both, part, part) if onward else (send, send, part, send)
    return pl.pallas_call(
        join_pass_kernel if onward else join_kernel,
        out_shape=shapes,
        in_specs=[VMEM, VMEM],
        out_specs=(VMEM,) * len(shapes),
        cost_estimate=SMALL,
        compiler_params=pltpu.CompilerParams(vmem_limit_bytes=8 * MIB),
        name="join_cores",
    )(keep, got)


def add_kernel(first_ref, got_ref, out_ref):
    tokens = first_ref.shape[0]
    out_ref[...] = (first_ref[...] + got_ref[tokens:, :].astype(F32)).astype(BF16)


def add(first, got):
    return pl.pallas_call(
        add_kernel,
        out_shape=jax.ShapeDtypeStruct(first.shape, BF16),
        in_specs=[VMEM, VMEM],
        out_specs=VMEM,
        cost_estimate=SMALL,
        compiler_params=pltpu.CompilerParams(vmem_limit_bytes=8 * MIB),
        name="add_planes",
    )(first, got)


def finish_kernel(picks, *refs):
    parts, (out_ref, gate_grad_ref) = refs[:-2], refs[-2:]
    tokens, width = out_ref.shape
    at = 0
    for p, group in enumerate((parts[:3], parts[3:])):
        total = group[0][...]
        for part in group[1:]:
            total = total + part[:tokens, :].astype(F32)
        cols = total.shape[1] - (0 if p else LANES)
        out_ref[:, at : at + cols] = total[:, :cols].astype(BF16)
        at += cols
        if not p:
            scores = total[:, cols : cols + picks].astype(BF16)
            gate_grad_ref[...] = lax.dot_general(
                scores, unit(tokens), TN, preferred_element_type=F32
            ).astype(BF16)


def finish(parts, width, picks):
    tokens = parts[0].shape[0]
    return pl.pallas_call(
        functools.partial(finish_kernel, picks),
        out_shape=(
            jax.ShapeDtypeStruct((tokens, width), BF16),
            jax.ShapeDtypeStruct((picks, tokens), BF16),
        ),
        in_specs=[VMEM] * len(parts),
        out_specs=(VMEM, VMEM),
        cost_estimate=SMALL,
        compiler_params=pltpu.CompilerParams(vmem_limit_bytes=8 * MIB),
        name="finish_tokens",
    )(*parts)


def relay_kernel(cuts, array_ref, *refs):
    outs, at = refs[-len(cuts) :], 0
    for cut, out in zip(cuts, outs):
        out[...] = array_ref[:, at : at + cut]
        at += cut


def relay(array, cuts, after):
    rows = array.shape[0]
    return pl.pallas_call(
        functools.partial(relay_kernel, cuts),
        out_shape=tuple(jax.ShapeDtypeStruct((rows, c), array.dtype) for c in cuts),
        in_specs=[VMEM] * (1 + len(after)),
        out_specs=(VMEM,) * len(cuts),
        cost_estimate=SMALL,
        compiler_params=pltpu.CompilerParams(vmem_limit_bytes=4 * MIB),
        name="relay",
    )(array, *(in_vmem(a) for a in after))


def swap(array, axis, mask):
    count = lax.axis_size(axis)
    return lax.ppermute(array, axis, [(i, i ^ mask) for i in range(count)])


def shards(out_grad, saved_input, routes, gate_int, w_gate, w_up, w_down):
    picks = routes.shape[1]
    chips = lax.axis_size("chip")
    width = saved_input.shape[1]
    cuts = (width + LANES, width)
    own = pack(saved_input, out_grad, routes.T, gate_int.T)
    far = swap(own, "far", 1)
    near = swap(own, "near", 1)
    beside = swap(own, "core", 1)
    def spread(blocks, after):
        sent = dispatch(blocks, chips, picks, after)
        return [sent[0]] + [swap(sent[j], "chip", j) for j in range(1, chips)]

    pair = ((own,), (beside,))
    first_rows = spread(pair, ())
    gate, up, gate_t, up_t = turn((w_gate[0], w_up[0]), first_rows[0])
    first = gather_rows(first_rows, ())
    (near,) = relay(near, (sum(cuts),), (gate_t, first))
    (far,) = relay(far, (sum(cuts),), (gate_t,))
    middle_pair = ((near,), (swap(near, "core", 1),), (far,), (swap(far, "core", 1),))
    across = relay(swap(far, "near", 1), cuts, ())
    across_pair = (across, tuple(swap(a, "core", 1) for a in across))
    middle_rows = spread(middle_pair, ())
    sent = list(dispatch(across_pair, chips, picks, ()))
    sums_of = lambda blocks: plan([b[0][:, width : width + LANES] for b in blocks], chips, picks)
    middle_sums, outer_sums = sums_of(middle_pair), sums_of(pair + across_pair)
    middle = gather_rows(middle_rows, (middle_sums[0], outer_sums[0]))
    (sent[-1],) = relay(sent[-1], (2 * width,), (middle,))
    last_rows = [sent[0]] + [swap(sent[j], "chip", j) for j in range(1, chips)]
    down_t = turn_only(w_down[0], last_rows[0])
    weights = (gate, up, gate_t, up_t, down_t)
    cols = min(1536, width // 2)
    early, part = expert(middle, first, last_rows, weights, cols)
    late = expert_rest(part, gate_t, up_t, cols, chips)
    parts = []
    for back in (early, late):
        rows = [back[0]] + [swap(back[j], "chip", j) for j in range(1, chips)]
        keep, send = combine((middle_sums, outer_sums), rows, picks, back is early)
        got = swap(send, "core", 1)
        if back is early:
            near, far, home = join(keep, got, True)
            near = swap(near, "near", 1)
            parts += [home, near, swap(add(far, near), "far", 1)]
        else:
            near, far, home, across = join(keep, got, False)
            parts += [home, swap(far, "far", 1), swap(across, ("far", "near"), 3), swap(near, "near", 1)]
    input_grad, gate_grad = finish(parts, width, picks)
    return input_grad, gate_grad.T


def solution(mesh):
    devices = mesh.devices
    split = Mesh(devices.reshape(2, 2, devices.size // 8, 2), AXES)
    rows, stack = P(AXES, None), P(AXES, None, None)
    return jax.shard_map(
        shards,
        mesh=split,
        in_specs=(rows,) * 4 + (stack,) * 3,
        out_specs=(rows, rows),
        check_vma=False,
    )
```

```python
import functools
import math

import jax
import jax.numpy as jnp
from jax import lax
from jax.experimental import pallas as pl
from jax.experimental.pallas import tpu as pltpu
from jax.sharding import Mesh
from jax.sharding import PartitionSpec as P

F32 = jnp.float32
BF16 = jnp.bfloat16
LANES = 128
SLOT = 4
AXES = ("far", "near", "chip", "core")
TN = (((0,), (0,)), ((), ()))
VMEM = pl.BlockSpec(memory_space=pltpu.VMEM)
HBM = pl.BlockSpec(memory_space=pltpu.HBM)
ANY = pl.BlockSpec(memory_space=pl.ANY)
MIB = 2**20
TAIL = 1024
PIECE = 256
SMALL = pl.CostEstimate(flops=1, bytes_accessed=1, transcendentals=0)


def iota(shape, dim):
    return lax.broadcasted_iota(jnp.int32, shape, dim)


def exact(mask):
    return mask.astype(F32).astype(BF16)


def in_hbm(array):
    return pltpu.with_memory_space_constraint(array, pltpu.HBM)


def in_vmem(array):
    return pltpu.with_memory_space_constraint(array, pltpu.VMEM)


def unit(count):
    return exact(iota((count, count), 0) == iota((count, count), 1))


def pack_kernel(input_hbm, grad_hbm, routes_hbm, gate_hbm, out_ref, routes_ref, gate_ref, sems):
    width = input_hbm.shape[1]
    copies = [
        pltpu.make_async_copy(routes_hbm, routes_ref, sems.at[0]),
        pltpu.make_async_copy(gate_hbm, gate_ref, sems.at[1]),
        pltpu.make_async_copy(input_hbm, out_ref.at[:, pl.ds(0, width)], sems.at[2]),
        pltpu.make_async_copy(grad_hbm, out_ref.at[:, pl.ds(width + LANES, width)], sems.at[3]),
    ]
    for copy in copies:
        copy.start()
    copies[0].wait()
    copies[1].wait()
    picks = routes_ref.shape[0]
    gate = gate_ref[...]
    table = jnp.concatenate([routes_ref[...], gate // 256, gate % 256], axis=0)
    place = exact(iota((3 * picks, LANES), 0) == iota((3 * picks, LANES), 1))
    out_ref[:, width : width + LANES] = lax.dot_general(
        table.astype(F32).astype(BF16), place, TN, preferred_element_type=F32
    ).astype(BF16)
    copies[2].wait()
    copies[3].wait()


def pack(input_rows, grad_rows, routes_t, gate_t):
    tokens, width = input_rows.shape
    return pl.pallas_call(
        pack_kernel,
        out_shape=jax.ShapeDtypeStruct((tokens, 2 * width + LANES), BF16),
        in_specs=[HBM] * 4,
        out_specs=VMEM,
        scratch_shapes=[
            pltpu.VMEM(routes_t.shape, jnp.int32),
            pltpu.VMEM(gate_t.shape, jnp.int32),
            pltpu.SemaphoreType.DMA((4,)),
        ],
        cost_estimate=SMALL,
        compiler_params=pltpu.CompilerParams(vmem_limit_bytes=4 * MIB),
        name="pack_tokens",
    )(*(in_hbm(a) for a in (input_rows, grad_rows, routes_t, gate_t)))


def choose(meta, chips, picks):
    tokens = meta[0].shape[0]
    blocks = len(meta)
    lines = blocks * SLOT
    names = jnp.concatenate([m[:, :picks] for m in meta], axis=0).astype(F32)
    shape = (blocks * tokens, chips * lines)
    lane, row = iota(shape, 1), iota(shape, 0)
    chip = jnp.bitwise_xor(lane // lines, lax.axis_index("chip"))
    plane = lax.axis_index("far") * 2 + lax.axis_index("near")
    owner = (2 * (plane * chips + chip) + lax.axis_index("core")).astype(F32)
    named = jnp.zeros(shape, F32)
    for k in range(picks):
        named = named + (names[:, k : k + 1] == owner).astype(F32)
    square = (blocks * tokens, blocks * tokens)
    r, c = iota(square, 0), iota(square, 1)
    before = exact(jnp.logical_and(c < r, c // tokens == r // tokens))
    rank = jnp.dot(before, named.astype(BF16), preferred_element_type=F32)
    fits = jnp.logical_and(rank == (lane % SLOT).astype(F32), (lane // SLOT) % blocks == row // tokens)
    return names, owner, jnp.where(fits, named, 0.0)


def dispatch_kernel(kinds, chips, picks, extra, *refs):
    outs = refs[-chips:]
    width = outs[0].shape[1] // 2
    blocks, at = [], 0
    for kind in kinds:
        if kind == 1:
            blocks.append((refs[at], refs[at], width + LANES))
        else:
            blocks.append((refs[at], refs[at + 1], 0))
        at += kind
    meta = [b[0][:, width : width + LANES] for b in blocks]
    _, _, hit = choose(meta, chips, picks)
    pick = hit.astype(BF16)
    lines = len(blocks) * SLOT
    step = math.gcd(width, 512)
    for part in range(2):
        for at in range(0, width, step):
            rows = jnp.concatenate(
                [
                    grads[:, first + at : first + at + step] if part else ins[:, at : at + step]
                    for ins, grads, first in blocks
                ],
                axis=0,
            )
            moved = lax.dot_general(pick, rows, TN, preferred_element_type=F32)
            for j in range(chips):
                outs[j][:, part * width + at : part * width + at + step] = moved[
                    j * lines : (j + 1) * lines, :
                ].astype(BF16)


def dispatch(blocks, chips, picks, after):
    kinds = tuple(len(b) for b in blocks)
    flat = [a for b in blocks for a in b]
    wide = sum(a.shape[1] for a in blocks[0]) - LANES
    lines = len(blocks) * SLOT
    return pl.pallas_call(
        functools.partial(dispatch_kernel, kinds, chips, picks, len(after)),
        out_shape=(jax.ShapeDtypeStruct((lines, wide), BF16),) * chips,
        in_specs=[VMEM] * (len(flat) + len(after)),
        out_specs=(VMEM,) * chips,
        cost_estimate=SMALL,
        compiler_params=pltpu.CompilerParams(vmem_limit_bytes=8 * MIB),
        name="dispatch_rows",
    )(*flat, *(in_vmem(a) for a in after))


def plan_kernel(chips, picks, *refs):
    meta, (weight_ref, mine_ref) = refs[:-2], refs[-2:]
    names, owner, hit = choose([m[...] for m in meta], chips, picks)
    tokens = names.shape[0]
    bytes_of = lambda part: jnp.concatenate(
        [m[:, part * picks : (part + 1) * picks] for m in meta], axis=0
    ).astype(F32)
    high, low = bytes_of(1) * (1.0 / 256.0), bytes_of(2) * (1.0 / 65536.0)
    high_weight, low_weight = jnp.zeros_like(hit), jnp.zeros_like(hit)
    for k in range(picks):
        same = jnp.where(names[:, k : k + 1] == owner, hit, 0.0)
        high_weight = high_weight + same * high[:, k : k + 1]
        low_weight = low_weight + same * low[:, k : k + 1]
        mine_ref[k * tokens : (k + 1) * tokens, :] = same.astype(BF16)
    weight_ref[:tokens, :] = high_weight.astype(BF16)
    weight_ref[tokens:, :] = low_weight.astype(BF16)


def plan(meta, chips, picks):
    tokens = len(meta) * meta[0].shape[0]
    rows = chips * len(meta) * SLOT
    return pl.pallas_call(
        functools.partial(plan_kernel, chips, picks),
        out_shape=(
            jax.ShapeDtypeStruct((2 * tokens, rows), BF16),
            jax.ShapeDtypeStruct((picks * tokens, rows), BF16),
        ),
        in_specs=[VMEM] * len(meta),
        out_specs=(VMEM, VMEM),
        cost_estimate=SMALL,
        compiler_params=pltpu.CompilerParams(vmem_limit_bytes=8 * MIB),
        name="plan_sums",
    )(*meta)


def turn_kernel(first, weight_ref, after_ref, turned):
    for at in range(0, turned.shape[1], PIECE):
        turned[:, pl.ds(at, PIECE)] = jnp.transpose(weight_ref[pl.ds(first + at, PIECE), :])


def turn(weight, first, rows, after):
    cols = weight.shape[1]
    return pl.pallas_call(
        functools.partial(turn_kernel, first),
        out_shape=pltpu.VMEM((cols, rows), BF16),
        in_specs=[VMEM, VMEM],
        out_specs=VMEM,
        cost_estimate=SMALL,
        compiler_params=pltpu.CompilerParams(vmem_limit_bytes=4 * MIB),
        name="turn_weight",
    )(in_vmem(weight), after)


def stack(refs, cut):
    return jnp.concatenate([r[:, cut].astype(F32) for r in refs], axis=0).astype(BF16)


def gather_kernel(count, extra, *refs):
    out_ref = refs[-1]
    wide = out_ref.shape[1]
    step = math.gcd(wide, 1024)
    for at in range(0, wide, step):
        out_ref[:, at : at + step] = stack(refs[:count], slice(at, at + step))


def gather_rows(arrays, after):
    count, (each, wide) = len(arrays), arrays[0].shape
    return pl.pallas_call(
        functools.partial(gather_kernel, count, len(after)),
        out_shape=jax.ShapeDtypeStruct((count * each, wide), BF16),
        in_specs=[VMEM] * (count + len(after)),
        out_specs=VMEM,
        cost_estimate=SMALL,
        compiler_params=pltpu.CompilerParams(vmem_limit_bytes=8 * MIB),
        name="gather_rows",
    )(*arrays, *after)


def by_chip(values, b, count):
    each = values.shape[0] // (4 * count)
    starts = (2 * each * b, 2 * each * count + each * b, 3 * each * count + each * b)
    return jnp.concatenate(
        [values[at : at + n] for at, n in zip(starts, (2 * each, each, each))], axis=0
    ).astype(BF16)


def row_tiles(gg_ref, gu_ref, gate_t_ref, up_t_ref, first, backs, width):
    for at in range(0, width, 512):
        step = min(512, width - at)
        cols = slice(first + at, first + at + step)
        row = jnp.dot(gg_ref[...], gate_t_ref[:, cols], preferred_element_type=F32)
        row = row + jnp.dot(gu_ref[...], up_t_ref[:, at : at + step], preferred_element_type=F32)
        for b, back in enumerate(backs):
            back[:, at : at + step] = by_chip(row, b, len(backs))


def expert_kernel(count, middle_ref, first_ref, *refs):
    arrived, rest_ref, refs = refs[:count], refs[count], refs[count + 1 :]
    gate_ref, up_ref, gate_t_ref, up_t_ref, down_t_ref = refs[:5]
    backs = refs[5 : 5 + count]
    gg_ref, gu_ref, rows_ref = refs[5 + count :]
    width, hidden = gate_ref.shape
    half, total = middle_ref.shape[0], 2 * middle_ref.shape[0]
    early = half + first_ref.shape[0]
    rows_ref[:half, :] = middle_ref[...]
    rows_ref[half:early, :] = first_ref[...]
    for at in range(0, 2 * width, 512):
        pieces = [(a, at) for a in arrived]
        if at >= arrived[-1].shape[1]:
            pieces[-1] = (rest_ref, at - arrived[-1].shape[1])
        rows_ref[early:, at : at + 512] = jnp.concatenate(
            [piece[:, first : first + 512].astype(F32) for piece, first in pieces], axis=0
        ).astype(BF16)
    score = jnp.zeros((total, 1), F32)
    for at in range(0, hidden, 512):
        cols = slice(at, min(at + 512, hidden))
        rows_in = rows_ref[:, :width]
        pre_gate = jnp.dot(rows_in, gate_ref[:, cols], preferred_element_type=F32)
        pre_up = jnp.dot(rows_in, up_ref[:, cols], preferred_element_type=F32)
        grad_hidden = jnp.dot(rows_ref[:, width:], down_t_ref[:, cols], preferred_element_type=F32)
        sigmoid = 1.0 / (1.0 + jnp.exp(-pre_gate))
        activated = pre_gate * sigmoid
        grad_up = grad_hidden * activated
        gg_ref[:, cols] = (
            grad_hidden * pre_up * sigmoid * (1.0 + pre_gate * (1.0 - sigmoid))
        ).astype(BF16)
        gu_ref[:, cols] = grad_up.astype(BF16)
        score = score + jnp.sum(grad_up * pre_up, axis=1, keepdims=True)
    score = jnp.broadcast_to(score, (total, LANES))
    cols = backs[0].shape[1] - LANES
    for b, back in enumerate(backs):
        back[:, cols:] = by_chip(score, b, count)
    row_tiles(gg_ref, gu_ref, gate_t_ref, up_t_ref, 0, backs, cols)


def expert(middle, first, arrived, weights, cols):
    width, hidden = weights[0].shape
    count, lines = len(arrived) - 1, 2 * arrived[0].shape[0]
    held = tuple(in_vmem(w) for w in weights)
    rows = 2 * count * lines
    part = jax.ShapeDtypeStruct((rows, hidden), BF16)
    outs = pl.pallas_call(
        functools.partial(expert_kernel, count),
        out_shape=(jax.ShapeDtypeStruct((2 * lines, cols + LANES), BF16),) * count + (part, part),
        in_specs=[VMEM] * (3 + count + len(held)),
        out_specs=(VMEM,) * (count + 2),
        scratch_shapes=[pltpu.VMEM((rows, 2 * width), BF16)],
        cost_estimate=SMALL,
        compiler_params=pltpu.CompilerParams(vmem_limit_bytes=max(8, rows // 20) * MIB),
        name="expert_rows",
    )(middle, first, *arrived, *held)
    return outs[:count], outs[count:]


def expert_rest_kernel(first, gg_ref, gu_ref, gate_t_ref, up_t_ref, *backs):
    row_tiles(gg_ref, gu_ref, gate_t_ref, up_t_ref, first, backs, backs[0].shape[1])


def expert_rest(part, gate_t, up_t, cols, count):
    lines = part[0].shape[0] // count
    return pl.pallas_call(
        functools.partial(expert_rest_kernel, cols),
        out_shape=(jax.ShapeDtypeStruct((lines, gate_t.shape[1] - cols), BF16),) * count,
        in_specs=[VMEM] * 4,
        out_specs=(VMEM,) * count,
        cost_estimate=SMALL,
        compiler_params=pltpu.CompilerParams(vmem_limit_bytes=8 * MIB),
        name="expert_rest",
    )(*part, in_vmem(gate_t), in_vmem(up_t))


def combine_kernel(picks, marked, *refs):
    weights, mines, refs = refs[:2], refs[2:4], refs[4:]
    backs, (keep_ref, send_ref) = refs[:-2], refs[-2:]
    lines, wide = backs[0].shape
    lines = lines // 2
    width = wide - LANES if marked else wide
    tokens = weights[0].shape[0] // 2
    own = tokens // 4

    def put(batch, values, cols):
        for z in range(2):
            at = (2 * batch + z) * own
            for side, ref in enumerate((keep_ref, send_ref)):
                first = (2 * z + side) * own
                ref[at : at + own, cols] = values[first : first + own, :]

    for batch in range(2):
        cut = slice(batch * lines, (batch + 1) * lines)
        for at in range(0, width, 512):
            cols = slice(at, min(at + 512, width))
            rows = jnp.concatenate([b[cut, cols] for b in backs], axis=0)
            total = jnp.dot(weights[batch][...], rows, preferred_element_type=F32)
            put(batch, (total[:tokens] + total[tokens:]).astype(BF16), cols)
        if marked:
            marks = jnp.concatenate([b[cut, width:] for b in backs], axis=0)
            value = jnp.dot(mines[batch][...], marks, preferred_element_type=F32)
            lane = iota((tokens, LANES), 1)
            spread = jnp.zeros((tokens, LANES), F32)
            for k in range(picks):
                spread = jnp.where(lane == k, value[k * tokens : (k + 1) * tokens, :], spread)
            put(batch, spread.astype(BF16), slice(width, wide))


def combine(sums, backs, picks, marked):
    tokens = sums[0][0].shape[0] // 2
    shape = jax.ShapeDtypeStruct((tokens, backs[0].shape[1]), BF16)
    return pl.pallas_call(
        functools.partial(combine_kernel, picks, marked),
        out_shape=(shape, shape),
        in_specs=[VMEM] * (4 + len(backs)),
        out_specs=(VMEM, VMEM),
        cost_estimate=SMALL,
        compiler_params=pltpu.CompilerParams(vmem_limit_bytes=8 * MIB),
        name="combine_rows",
    )(sums[0][0], sums[1][0], sums[0][1], sums[1][1], *backs)


def join_kernel(keep_ref, got_ref, *outs):
    tokens = outs[0].shape[0]
    total = keep_ref[...].astype(F32) + got_ref[...].astype(F32)
    for z, out in enumerate(outs):
        out[...] = total[z * tokens : (z + 1) * tokens, :].astype(out.dtype)


def join_pass_kernel(keep_ref, got_ref, near_ref, far_ref, home_ref):
    tokens = home_ref.shape[0]
    total = keep_ref[...].astype(F32) + got_ref[...].astype(F32)
    near_ref[:tokens, :] = total[:tokens, :].astype(BF16)
    far_ref[...] = total[tokens : 2 * tokens, :]
    home_ref[...] = total[2 * tokens : 3 * tokens, :]
    near_ref[tokens:, :] = total[3 * tokens :, :].astype(BF16)


def join(keep, got, onward):
    tokens, cols = keep.shape[0] // 4, keep.shape[1]
    part = jax.ShapeDtypeStruct((tokens, cols), F32)
    send = jax.ShapeDtypeStruct((tokens, cols), BF16)
    both = jax.ShapeDtypeStruct((2 * tokens, cols), BF16)
    shapes = (both, part, part) if onward else (send, send, part, send)
    return pl.pallas_call(
        join_pass_kernel if onward else join_kernel,
        out_shape=shapes,
        in_specs=[VMEM, VMEM],
        out_specs=(VMEM,) * len(shapes),
        cost_estimate=SMALL,
        compiler_params=pltpu.CompilerParams(vmem_limit_bytes=8 * MIB),
        name="join_cores",
    )(keep, got)


def add_kernel(first_ref, got_ref, out_ref):
    tokens = first_ref.shape[0]
    out_ref[...] = (first_ref[...] + got_ref[tokens:, :].astype(F32)).astype(BF16)


def add(first, got):
    return pl.pallas_call(
        add_kernel,
        out_shape=jax.ShapeDtypeStruct(first.shape, BF16),
        in_specs=[VMEM, VMEM],
        out_specs=VMEM,
        cost_estimate=SMALL,
        compiler_params=pltpu.CompilerParams(vmem_limit_bytes=8 * MIB),
        name="add_planes",
    )(first, got)


def finish_kernel(picks, *refs):
    parts, (out_ref, gate_grad_ref) = refs[:-2], refs[-2:]
    tokens, width = out_ref.shape
    at = 0
    for p, group in enumerate((parts[:3], parts[3:])):
        total = group[0][...]
        for part in group[1:]:
            total = total + part[:tokens, :].astype(F32)
        cols = total.shape[1] - (0 if p else LANES)
        out_ref[:, at : at + cols] = total[:, :cols].astype(BF16)
        at += cols
        if not p:
            scores = total[:, cols : cols + picks].astype(BF16)
            gate_grad_ref[...] = lax.dot_general(
                scores, unit(tokens), TN, preferred_element_type=F32
            ).astype(BF16)


def finish(parts, width, picks):
    tokens = parts[0].shape[0]
    return pl.pallas_call(
        functools.partial(finish_kernel, picks),
        out_shape=(
            jax.ShapeDtypeStruct((tokens, width), BF16),
            jax.ShapeDtypeStruct((picks, tokens), BF16),
        ),
        in_specs=[VMEM] * len(parts),
        out_specs=(VMEM, VMEM),
        cost_estimate=SMALL,
        compiler_params=pltpu.CompilerParams(vmem_limit_bytes=8 * MIB),
        name="finish_tokens",
    )(*parts)


def relay_kernel(cuts, array_ref, *refs):
    outs, at = refs[-len(cuts) :], 0
    for cut, out in zip(cuts, outs):
        out[...] = array_ref[:, at : at + cut]
        at += cut


def relay(array, cuts, after):
    rows = array.shape[0]
    return pl.pallas_call(
        functools.partial(relay_kernel, cuts),
        out_shape=tuple(jax.ShapeDtypeStruct((rows, c), array.dtype) for c in cuts),
        in_specs=[VMEM] * (1 + len(after)),
        out_specs=(VMEM,) * len(cuts),
        cost_estimate=SMALL,
        compiler_params=pltpu.CompilerParams(vmem_limit_bytes=4 * MIB),
        name="relay",
    )(array, *(in_vmem(a) for a in after))


def swap(array, axis, mask):
    count = lax.axis_size(axis)
    return lax.ppermute(array, axis, [(i, i ^ mask) for i in range(count)])


def shards(out_grad, saved_input, routes, gate_int, w_gate, w_up, w_down):
    picks = routes.shape[1]
    chips = lax.axis_size("chip")
    width = saved_input.shape[1]
    cuts = (width + LANES, width)
    own = pack(saved_input, out_grad, routes.T, gate_int.T)
    far = swap(own, "far", 1)
    near = swap(own, "near", 1)
    beside = swap(own, "core", 1)
    def spread(blocks, after):
        sent = dispatch(blocks, chips, picks, after)
        return [sent[0]] + [swap(sent[j], "chip", j) for j in range(1, chips)]

    pair = ((own,), (beside,))
    first_rows = spread(pair, ())
    cols = min(1536, width // 2)
    gate, up, down = w_gate[0], w_up[0], w_down[0]
    gate_t = turn(gate, 0, width, first_rows[0])
    first = gather_rows(first_rows, ())
    (near,) = relay(near, (sum(cuts),), (gate_t, first))
    (far,) = relay(far, (sum(cuts),), (gate_t,))
    middle_pair = ((near,), (swap(near, "core", 1),), (far,), (swap(far, "core", 1),))
    middle_sent = dispatch(middle_pair, chips, picks, ())
    middle_rows = [middle_sent[0]] + [swap(middle_sent[j], "chip", j) for j in range(1, chips)]
    up_t_b = turn(up, cols, width - cols, middle_sent[0])
    across = relay(swap(far, "near", 1), cuts, (up_t_b,))
    across_pair = (across, tuple(swap(a, "core", 1) for a in across))
    sent = list(dispatch(across_pair, chips, picks, ()))
    sums_of = lambda blocks: plan([b[0][:, width : width + LANES] for b in blocks], chips, picks)
    middle_sums, outer_sums = sums_of(middle_pair), sums_of(pair + across_pair)
    up_t_a = turn(up, 0, cols, sent[0])
    middle = gather_rows(middle_rows, (middle_sums[0], outer_sums[0], in_vmem(up_t_a)))
    tail = min(TAIL, width)
    sent[-1], rest = relay(sent[-1], (2 * width - tail, tail), ())
    (rest,) = relay(rest, (tail,), (middle,))
    last_rows = [sent[0]] + [swap(sent[j], "chip", j) for j in range(1, chips)]
    last_rows.append(swap(rest, "chip", chips - 1))
    down_t = turn(down, 0, down.shape[0], rest)
    weights = (gate, up, gate_t, up_t_a, down_t)
    early, part = expert(middle, first, last_rows, weights, cols)
    late = expert_rest(part, gate_t, up_t_b, cols, chips)
    parts = []
    for back in (early, late):
        rows = [back[0]] + [swap(back[j], "chip", j) for j in range(1, chips)]
        keep, send = combine((middle_sums, outer_sums), rows, picks, back is early)
        got = swap(send, "core", 1)
        if back is early:
            near, far, home = join(keep, got, True)
            near = swap(near, "near", 1)
            parts += [home, near, swap(add(far, near), "far", 1)]
        else:
            near, far, home, across = join(keep, got, False)
            parts += [home, swap(far, "far", 1), swap(across, ("far", "near"), 3), swap(near, "near", 1)]
    input_grad, gate_grad = finish(parts, width, picks)
    return input_grad, gate_grad.T


def solution(mesh):
    devices = mesh.devices
    split = Mesh(devices.reshape(2, 2, devices.size // 8, 2), AXES)
    rows, stack = P(AXES, None), P(AXES, None, None)
    return jax.shard_map(
        shards,
        mesh=split,
        in_specs=(rows,) * 4 + (stack,) * 3,
        out_specs=(rows, rows),
        check_vma=False,
    )
```

```python
import functools
import math

import jax
import jax.numpy as jnp
from jax import lax
from jax.experimental import pallas as pl
from jax.experimental.pallas import tpu as pltpu
from jax.sharding import Mesh
from jax.sharding import PartitionSpec as P

F32 = jnp.float32
BF16 = jnp.bfloat16
LANES = 128
SLOT = 4
AXES = ("far", "near", "chip", "core")
TN = (((0,), (0,)), ((), ()))
VMEM = pl.BlockSpec(memory_space=pltpu.VMEM)
HBM = pl.BlockSpec(memory_space=pltpu.HBM)
ANY = pl.BlockSpec(memory_space=pl.ANY)
MIB = 2**20
TAIL = 1024
CUT = 2
PIECE = 256
SMALL = pl.CostEstimate(flops=1, bytes_accessed=1, transcendentals=0)


def iota(shape, dim):
    return lax.broadcasted_iota(jnp.int32, shape, dim)


def exact(mask):
    return mask.astype(F32).astype(BF16)


def in_hbm(array):
    return pltpu.with_memory_space_constraint(array, pltpu.HBM)


def in_vmem(array):
    return pltpu.with_memory_space_constraint(array, pltpu.VMEM)


def unit(count):
    return exact(iota((count, count), 0) == iota((count, count), 1))


def pack_kernel(input_hbm, grad_hbm, routes_hbm, gate_hbm, out_ref, routes_ref, gate_ref, sems):
    width = input_hbm.shape[1]
    copies = [
        pltpu.make_async_copy(routes_hbm, routes_ref, sems.at[0]),
        pltpu.make_async_copy(gate_hbm, gate_ref, sems.at[1]),
        pltpu.make_async_copy(input_hbm, out_ref.at[:, pl.ds(0, width)], sems.at[2]),
        pltpu.make_async_copy(grad_hbm, out_ref.at[:, pl.ds(width + LANES, width)], sems.at[3]),
    ]
    for copy in copies:
        copy.start()
    copies[0].wait()
    copies[1].wait()
    picks = routes_ref.shape[0]
    gate = gate_ref[...]
    table = jnp.concatenate([routes_ref[...], gate // 256, gate % 256], axis=0)
    place = exact(iota((3 * picks, LANES), 0) == iota((3 * picks, LANES), 1))
    out_ref[:, width : width + LANES] = lax.dot_general(
        table.astype(F32).astype(BF16), place, TN, preferred_element_type=F32
    ).astype(BF16)
    copies[2].wait()
    copies[3].wait()


def pack(input_rows, grad_rows, routes_t, gate_t):
    tokens, width = input_rows.shape
    return pl.pallas_call(
        pack_kernel,
        out_shape=jax.ShapeDtypeStruct((tokens, 2 * width + LANES), BF16),
        in_specs=[HBM] * 4,
        out_specs=VMEM,
        scratch_shapes=[
            pltpu.VMEM(routes_t.shape, jnp.int32),
            pltpu.VMEM(gate_t.shape, jnp.int32),
            pltpu.SemaphoreType.DMA((4,)),
        ],
        cost_estimate=SMALL,
        compiler_params=pltpu.CompilerParams(vmem_limit_bytes=4 * MIB),
        name="pack_tokens",
    )(*(in_hbm(a) for a in (input_rows, grad_rows, routes_t, gate_t)))


def choose(meta, chips, picks):
    tokens = meta[0].shape[0]
    blocks = len(meta)
    lines = blocks * SLOT
    names = jnp.concatenate([m[:, :picks] for m in meta], axis=0).astype(F32)
    shape = (blocks * tokens, chips * lines)
    lane, row = iota(shape, 1), iota(shape, 0)
    chip = jnp.bitwise_xor(lane // lines, lax.axis_index("chip"))
    plane = lax.axis_index("far") * 2 + lax.axis_index("near")
    owner = (2 * (plane * chips + chip) + lax.axis_index("core")).astype(F32)
    named = jnp.zeros(shape, F32)
    for k in range(picks):
        named = named + (names[:, k : k + 1] == owner).astype(F32)
    square = (blocks * tokens, blocks * tokens)
    r, c = iota(square, 0), iota(square, 1)
    before = exact(jnp.logical_and(c < r, c // tokens == r // tokens))
    rank = jnp.dot(before, named.astype(BF16), preferred_element_type=F32)
    fits = jnp.logical_and(rank == (lane % SLOT).astype(F32), (lane // SLOT) % blocks == row // tokens)
    return names, owner, jnp.where(fits, named, 0.0)


def dispatch_kernel(kinds, chips, picks, extra, *refs):
    outs = refs[-chips:]
    width = outs[0].shape[1] // 2
    blocks, at = [], 0
    for kind in kinds:
        if kind == 1:
            blocks.append((refs[at], refs[at], width + LANES))
        else:
            blocks.append((refs[at], refs[at + 1], 0))
        at += kind
    meta = [b[0][:, width : width + LANES] for b in blocks]
    _, _, hit = choose(meta, chips, picks)
    pick = hit.astype(BF16)
    lines = len(blocks) * SLOT
    step = math.gcd(width, 512)
    for part in range(2):
        for at in range(0, width, step):
            rows = jnp.concatenate(
                [
                    grads[:, first + at : first + at + step] if part else ins[:, at : at + step]
                    for ins, grads, first in blocks
                ],
                axis=0,
            )
            moved = lax.dot_general(pick, rows, TN, preferred_element_type=F32)
            for j in range(chips):
                outs[j][:, part * width + at : part * width + at + step] = moved[
                    j * lines : (j + 1) * lines, :
                ].astype(BF16)


def dispatch(blocks, chips, picks, after):
    kinds = tuple(len(b) for b in blocks)
    flat = [a for b in blocks for a in b]
    wide = sum(a.shape[1] for a in blocks[0]) - LANES
    lines = len(blocks) * SLOT
    return pl.pallas_call(
        functools.partial(dispatch_kernel, kinds, chips, picks, len(after)),
        out_shape=(jax.ShapeDtypeStruct((lines, wide), BF16),) * chips,
        in_specs=[VMEM] * (len(flat) + len(after)),
        out_specs=(VMEM,) * chips,
        cost_estimate=SMALL,
        compiler_params=pltpu.CompilerParams(vmem_limit_bytes=8 * MIB),
        name="dispatch_rows",
    )(*flat, *(in_vmem(a) for a in after))


def plan_kernel(chips, picks, *refs):
    meta, (weight_ref, mine_ref) = refs[:-2], refs[-2:]
    names, owner, hit = choose([m[...] for m in meta], chips, picks)
    tokens = names.shape[0]
    bytes_of = lambda part: jnp.concatenate(
        [m[:, part * picks : (part + 1) * picks] for m in meta], axis=0
    ).astype(F32)
    high, low = bytes_of(1) * (1.0 / 256.0), bytes_of(2) * (1.0 / 65536.0)
    high_weight, low_weight = jnp.zeros_like(hit), jnp.zeros_like(hit)
    for k in range(picks):
        same = jnp.where(names[:, k : k + 1] == owner, hit, 0.0)
        high_weight = high_weight + same * high[:, k : k + 1]
        low_weight = low_weight + same * low[:, k : k + 1]
        mine_ref[k * tokens : (k + 1) * tokens, :] = same.astype(BF16)
    weight_ref[:tokens, :] = high_weight.astype(BF16)
    weight_ref[tokens:, :] = low_weight.astype(BF16)


def plan(meta, chips, picks):
    tokens = len(meta) * meta[0].shape[0]
    rows = chips * len(meta) * SLOT
    return pl.pallas_call(
        functools.partial(plan_kernel, chips, picks),
        out_shape=(
            jax.ShapeDtypeStruct((2 * tokens, rows), BF16),
            jax.ShapeDtypeStruct((picks * tokens, rows), BF16),
        ),
        in_specs=[VMEM] * len(meta),
        out_specs=(VMEM, VMEM),
        cost_estimate=SMALL,
        compiler_params=pltpu.CompilerParams(vmem_limit_bytes=8 * MIB),
        name="plan_sums",
    )(*meta)


def turn_kernel(first, weight_ref, after_ref, turned):
    for at in range(0, turned.shape[1], PIECE):
        turned[:, pl.ds(at, PIECE)] = jnp.transpose(weight_ref[pl.ds(first + at, PIECE), :])


def turn(weight, first, rows, after):
    cols = weight.shape[1]
    return pl.pallas_call(
        functools.partial(turn_kernel, first),
        out_shape=pltpu.VMEM((cols, rows), BF16),
        in_specs=[VMEM, VMEM],
        out_specs=VMEM,
        cost_estimate=SMALL,
        compiler_params=pltpu.CompilerParams(vmem_limit_bytes=4 * MIB),
        name="turn_weight",
    )(in_vmem(weight), after)


def stack(refs, cut):
    return jnp.concatenate([r[:, cut].astype(F32) for r in refs], axis=0).astype(BF16)


def gather_kernel(count, extra, *refs):
    out_ref = refs[-1]
    wide = out_ref.shape[1]
    step = math.gcd(wide, 1024)
    for at in range(0, wide, step):
        out_ref[:, at : at + step] = stack(refs[:count], slice(at, at + step))


def gather_rows(arrays, after):
    count, (each, wide) = len(arrays), arrays[0].shape
    return pl.pallas_call(
        functools.partial(gather_kernel, count, len(after)),
        out_shape=jax.ShapeDtypeStruct((count * each, wide), BF16),
        in_specs=[VMEM] * (count + len(after)),
        out_specs=VMEM,
        cost_estimate=SMALL,
        compiler_params=pltpu.CompilerParams(vmem_limit_bytes=8 * MIB),
        name="gather_rows",
    )(*arrays, *after)


def by_chip(values, b, count):
    each = values.shape[0] // (4 * count)
    starts = (2 * each * b, 2 * each * count + each * b, 3 * each * count + each * b)
    return jnp.concatenate(
        [values[at : at + n] for at, n in zip(starts, (2 * each, each, each))], axis=0
    ).astype(BF16)


def row_tiles(gg_ref, gu_ref, gate_t_ref, up_t_ref, first, backs, width):
    for at in range(0, width, 512):
        step = min(512, width - at)
        cols = slice(first + at, first + at + step)
        row = jnp.dot(gg_ref[...], gate_t_ref[:, cols], preferred_element_type=F32)
        row = row + jnp.dot(gu_ref[...], up_t_ref[:, at : at + step], preferred_element_type=F32)
        for b, back in enumerate(backs):
            back[:, at : at + step] = by_chip(row, b, len(backs))


def expert_kernel(count, middle_ref, first_ref, *refs):
    arrived, rest_ref, refs = refs[:count], refs[count], refs[count + 1 :]
    gate_ref, up_ref, gate_t_ref, up_t_ref, down_t_ref = refs[:5]
    backs = refs[5 : 5 + count]
    gg_ref, gu_ref, rows_ref = refs[5 + count :]
    width, hidden = gate_ref.shape
    half, total = middle_ref.shape[0], 2 * middle_ref.shape[0]
    early = half + first_ref.shape[0]
    rows_ref[:half, :] = middle_ref[...]
    rows_ref[half:early, :] = first_ref[...]
    for at in range(0, 2 * width, 512):
        pieces = [(a, at) for a in arrived]
        if at >= arrived[CUT].shape[1]:
            pieces[CUT] = (rest_ref, at - arrived[CUT].shape[1])
        rows_ref[early:, at : at + 512] = jnp.concatenate(
            [piece[:, first : first + 512].astype(F32) for piece, first in pieces], axis=0
        ).astype(BF16)
    score = jnp.zeros((total, 1), F32)
    for at in range(0, hidden, 512):
        cols = slice(at, min(at + 512, hidden))
        rows_in = rows_ref[:, :width]
        pre_gate = jnp.dot(rows_in, gate_ref[:, cols], preferred_element_type=F32)
        pre_up = jnp.dot(rows_in, up_ref[:, cols], preferred_element_type=F32)
        grad_hidden = jnp.dot(rows_ref[:, width:], down_t_ref[:, cols], preferred_element_type=F32)
        sigmoid = 1.0 / (1.0 + jnp.exp(-pre_gate))
        activated = pre_gate * sigmoid
        grad_up = grad_hidden * activated
        gg_ref[:, cols] = (
            grad_hidden * pre_up * sigmoid * (1.0 + pre_gate * (1.0 - sigmoid))
        ).astype(BF16)
        gu_ref[:, cols] = grad_up.astype(BF16)
        score = score + jnp.sum(grad_up * pre_up, axis=1, keepdims=True)
    score = jnp.broadcast_to(score, (total, LANES))
    cols = backs[0].shape[1] - LANES
    for b, back in enumerate(backs):
        back[:, cols:] = by_chip(score, b, count)
    row_tiles(gg_ref, gu_ref, gate_t_ref, up_t_ref, 0, backs, cols)


def expert(middle, first, arrived, weights, cols):
    width, hidden = weights[0].shape
    count, lines = len(arrived) - 1, 2 * arrived[0].shape[0]
    held = tuple(in_vmem(w) for w in weights)
    rows = 2 * count * lines
    part = jax.ShapeDtypeStruct((rows, hidden), BF16)
    outs = pl.pallas_call(
        functools.partial(expert_kernel, count),
        out_shape=(jax.ShapeDtypeStruct((2 * lines, cols + LANES), BF16),) * count + (part, part),
        in_specs=[VMEM] * (3 + count + len(held)),
        out_specs=(VMEM,) * (count + 2),
        scratch_shapes=[pltpu.VMEM((rows, 2 * width), BF16)],
        cost_estimate=SMALL,
        compiler_params=pltpu.CompilerParams(vmem_limit_bytes=max(8, rows // 20) * MIB),
        name="expert_rows",
    )(middle, first, *arrived, *held)
    return outs[:count], outs[count:]


def expert_rest_kernel(first, gg_ref, gu_ref, gate_t_ref, up_t_ref, *backs):
    row_tiles(gg_ref, gu_ref, gate_t_ref, up_t_ref, first, backs, backs[0].shape[1])


def expert_rest(part, gate_t, up_t, cols, count):
    lines = part[0].shape[0] // count
    return pl.pallas_call(
        functools.partial(expert_rest_kernel, cols),
        out_shape=(jax.ShapeDtypeStruct((lines, gate_t.shape[1] - cols), BF16),) * count,
        in_specs=[VMEM] * 4,
        out_specs=(VMEM,) * count,
        cost_estimate=SMALL,
        compiler_params=pltpu.CompilerParams(vmem_limit_bytes=8 * MIB),
        name="expert_rest",
    )(*part, in_vmem(gate_t), in_vmem(up_t))


def combine_kernel(picks, marked, *refs):
    weights, mines, refs = refs[:2], refs[2:4], refs[4:]
    backs, (keep_ref, send_ref) = refs[:-2], refs[-2:]
    lines, wide = backs[0].shape
    lines = lines // 2
    width = wide - LANES if marked else wide
    tokens = weights[0].shape[0] // 2
    own = tokens // 4

    def put(batch, values, cols):
        for z in range(2):
            at = (2 * batch + z) * own
            for side, ref in enumerate((keep_ref, send_ref)):
                first = (2 * z + side) * own
                ref[at : at + own, cols] = values[first : first + own, :]

    for batch in range(2):
        cut = slice(batch * lines, (batch + 1) * lines)
        for at in range(0, width, 512):
            cols = slice(at, min(at + 512, width))
            rows = jnp.concatenate([b[cut, cols] for b in backs], axis=0)
            total = jnp.dot(weights[batch][...], rows, preferred_element_type=F32)
            put(batch, (total[:tokens] + total[tokens:]).astype(BF16), cols)
        if marked:
            marks = jnp.concatenate([b[cut, width:] for b in backs], axis=0)
            value = jnp.dot(mines[batch][...], marks, preferred_element_type=F32)
            lane = iota((tokens, LANES), 1)
            spread = jnp.zeros((tokens, LANES), F32)
            for k in range(picks):
                spread = jnp.where(lane == k, value[k * tokens : (k + 1) * tokens, :], spread)
            put(batch, spread.astype(BF16), slice(width, wide))


def combine(sums, backs, picks, marked):
    tokens = sums[0][0].shape[0] // 2
    shape = jax.ShapeDtypeStruct((tokens, backs[0].shape[1]), BF16)
    return pl.pallas_call(
        functools.partial(combine_kernel, picks, marked),
        out_shape=(shape, shape),
        in_specs=[VMEM] * (4 + len(backs)),
        out_specs=(VMEM, VMEM),
        cost_estimate=SMALL,
        compiler_params=pltpu.CompilerParams(vmem_limit_bytes=8 * MIB),
        name="combine_rows",
    )(sums[0][0], sums[1][0], sums[0][1], sums[1][1], *backs)


def join_kernel(keep_ref, got_ref, *outs):
    tokens = outs[0].shape[0]
    total = keep_ref[...].astype(F32) + got_ref[...].astype(F32)
    for z, out in enumerate(outs):
        out[...] = total[z * tokens : (z + 1) * tokens, :].astype(out.dtype)


def join_pass_kernel(keep_ref, got_ref, near_ref, far_ref, home_ref):
    tokens = home_ref.shape[0]
    total = keep_ref[...].astype(F32) + got_ref[...].astype(F32)
    near_ref[:tokens, :] = total[:tokens, :].astype(BF16)
    far_ref[...] = total[tokens : 2 * tokens, :]
    home_ref[...] = total[2 * tokens : 3 * tokens, :]
    near_ref[tokens:, :] = total[3 * tokens :, :].astype(BF16)


def join(keep, got, onward):
    tokens, cols = keep.shape[0] // 4, keep.shape[1]
    part = jax.ShapeDtypeStruct((tokens, cols), F32)
    send = jax.ShapeDtypeStruct((tokens, cols), BF16)
    both = jax.ShapeDtypeStruct((2 * tokens, cols), BF16)
    shapes = (both, part, part) if onward else (send, send, part, send)
    return pl.pallas_call(
        join_pass_kernel if onward else join_kernel,
        out_shape=shapes,
        in_specs=[VMEM, VMEM],
        out_specs=(VMEM,) * len(shapes),
        cost_estimate=SMALL,
        compiler_params=pltpu.CompilerParams(vmem_limit_bytes=8 * MIB),
        name="join_cores",
    )(keep, got)


def add_kernel(first_ref, got_ref, out_ref):
    tokens = first_ref.shape[0]
    out_ref[...] = (first_ref[...] + got_ref[tokens:, :].astype(F32)).astype(BF16)


def add(first, got):
    return pl.pallas_call(
        add_kernel,
        out_shape=jax.ShapeDtypeStruct(first.shape, BF16),
        in_specs=[VMEM, VMEM],
        out_specs=VMEM,
        cost_estimate=SMALL,
        compiler_params=pltpu.CompilerParams(vmem_limit_bytes=8 * MIB),
        name="add_planes",
    )(first, got)


def finish_kernel(picks, *refs):
    parts, (out_ref, gate_grad_ref) = refs[:-2], refs[-2:]
    tokens, width = out_ref.shape
    at = 0
    for p, group in enumerate((parts[:3], parts[3:])):
        total = group[0][...]
        for part in group[1:]:
            total = total + part[:tokens, :].astype(F32)
        cols = total.shape[1] - (0 if p else LANES)
        out_ref[:, at : at + cols] = total[:, :cols].astype(BF16)
        at += cols
        if not p:
            scores = total[:, cols : cols + picks].astype(BF16)
            gate_grad_ref[...] = lax.dot_general(
                scores, unit(tokens), TN, preferred_element_type=F32
            ).astype(BF16)


def finish(parts, width, picks):
    tokens = parts[0].shape[0]
    return pl.pallas_call(
        functools.partial(finish_kernel, picks),
        out_shape=(
            jax.ShapeDtypeStruct((tokens, width), BF16),
            jax.ShapeDtypeStruct((picks, tokens), BF16),
        ),
        in_specs=[VMEM] * len(parts),
        out_specs=(VMEM, VMEM),
        cost_estimate=SMALL,
        compiler_params=pltpu.CompilerParams(vmem_limit_bytes=8 * MIB),
        name="finish_tokens",
    )(*parts)


def relay_kernel(cuts, array_ref, *refs):
    outs, at = refs[-len(cuts) :], 0
    for cut, out in zip(cuts, outs):
        out[...] = array_ref[:, at : at + cut]
        at += cut


def relay(array, cuts, after):
    rows = array.shape[0]
    return pl.pallas_call(
        functools.partial(relay_kernel, cuts),
        out_shape=tuple(jax.ShapeDtypeStruct((rows, c), array.dtype) for c in cuts),
        in_specs=[VMEM] * (1 + len(after)),
        out_specs=(VMEM,) * len(cuts),
        cost_estimate=SMALL,
        compiler_params=pltpu.CompilerParams(vmem_limit_bytes=4 * MIB),
        name="relay",
    )(array, *(in_vmem(a) for a in after))


def swap(array, axis, mask):
    count = lax.axis_size(axis)
    return lax.ppermute(array, axis, [(i, i ^ mask) for i in range(count)])


def shards(out_grad, saved_input, routes, gate_int, w_gate, w_up, w_down):
    picks = routes.shape[1]
    chips = lax.axis_size("chip")
    width = saved_input.shape[1]
    cuts = (width + LANES, width)
    own = pack(saved_input, out_grad, routes.T, gate_int.T)
    far = swap(own, "far", 1)
    near = swap(own, "near", 1)
    beside = swap(own, "core", 1)
    def spread(blocks, after):
        sent = dispatch(blocks, chips, picks, after)
        return [sent[0]] + [swap(sent[j], "chip", j) for j in range(1, chips)]

    pair = ((own,), (beside,))
    first_rows = spread(pair, ())
    cols = min(1536, width // 2)
    gate, up, down = w_gate[0], w_up[0], w_down[0]
    gate_t = turn(gate, 0, width, first_rows[0])
    first = gather_rows(first_rows, ())
    (near,) = relay(near, (sum(cuts),), (gate_t, first))
    (far,) = relay(far, (sum(cuts),), (gate_t,))
    middle_pair = ((near,), (swap(near, "core", 1),), (far,), (swap(far, "core", 1),))
    middle_sent = dispatch(middle_pair, chips, picks, ())
    middle_rows = [middle_sent[0]] + [swap(middle_sent[j], "chip", j) for j in range(1, chips)]
    up_t_b = turn(up, cols, width - cols, middle_sent[0])
    across = relay(swap(far, "near", 1), cuts, (up_t_b,))
    across_pair = (across, tuple(swap(a, "core", 1) for a in across))
    sent = list(dispatch(across_pair, chips, picks, ()))
    sums_of = lambda blocks: plan([b[0][:, width : width + LANES] for b in blocks], chips, picks)
    middle_sums, outer_sums = sums_of(middle_pair), sums_of(pair + across_pair)
    up_t_a = turn(up, 0, cols, sent[0])
    middle = gather_rows(middle_rows, (middle_sums[0], outer_sums[0], in_vmem(up_t_a)))
    tail = min(TAIL, width)
    sent[CUT], rest = relay(sent[CUT], (2 * width - tail, tail), ())
    (rest,) = relay(rest, (tail,), (middle,))
    last_rows = [sent[0]] + [swap(sent[j], "chip", j) for j in range(1, chips)]
    last_rows.append(swap(rest, "chip", CUT))
    down_t = turn(down, 0, down.shape[0], rest)
    weights = (gate, up, gate_t, up_t_a, down_t)
    early, part = expert(middle, first, last_rows, weights, cols)
    late = expert_rest(part, gate_t, up_t_b, cols, chips)
    parts = []
    for back in (early, late):
        rows = [back[0]] + [swap(back[j], "chip", j) for j in range(1, chips)]
        keep, send = combine((middle_sums, outer_sums), rows, picks, back is early)
        got = swap(send, "core", 1)
        if back is early:
            near, far, home = join(keep, got, True)
            near = swap(near, "near", 1)
            parts += [home, near, swap(add(far, near), "far", 1)]
        else:
            near, far, home, across = join(keep, got, False)
            parts += [home, swap(far, "far", 1), swap(across, ("far", "near"), 3), swap(near, "near", 1)]
    input_grad, gate_grad = finish(parts, width, picks)
    return input_grad, gate_grad.T


def solution(mesh):
    devices = mesh.devices
    split = Mesh(devices.reshape(2, 2, devices.size // 8, 2), AXES)
    rows, stack = P(AXES, None), P(AXES, None, None)
    return jax.shard_map(
        shards,
        mesh=split,
        in_specs=(rows,) * 4 + (stack,) * 3,
        out_specs=(rows, rows),
        check_vma=False,
    )
```
